32 devices in a mesh: space: 8 (over y, x, core), help: 4 (over z).
Axes of the slice: x: 2, y: 2, z: 4, core: 2. Of those that a mesh axis runs over, the one named last changes fastest.
Arguments:
- solution: float32 [9, 4096, 512], P(None, ('space', 'help')), may hold values from -6 to 6
- material: float32 [3, 4096, 512], P(None, ('space', 'help')), may hold values from 0.5 to 2
- neighbours: int32 [6, 4096], P(None, ('space', 'help')), may hold values from 0 to 4095, as said below
- refine_count: int32 [8, 4], P('space', 'help'), may hold values from 1 to 64, 128 in all within a row
Outputs:
- evolved: float32 [9, 4096, 512], P(None, ('space', 'help'))
The draws below stay inside these ranges and needn't reach their ends.
Inputs may be any that keep to these rules, and one draw needn't show every extreme that they name: The neighbours across y and z faces lie on the same device; across x+ on the device next along space (index + 1, wrapping) with the same help index, across x- on the previous one. Neighbours are mutual: the x+ neighbour's x- neighbour is the cell itself, likewise for y and z. `refine_count`: A device's cells whose index within the device is under its count are refined; the counts of one help group sum to 128.
All inputs are finite; a program needn't handle non-finite values.
Results may differ from the reference program's by a relative error of at most 0.0001.
Values sent between devices are 32-bit elements; how exact they have to be, the bound alone decides.
No kernel may reach another device: no remote copies, remote signals or barrier semaphores. Data moves between devices by JAX's collectives and lax.ppermute only.
A program may use at most 128 MiB of HBM per device.

```python
import math
import jax
import jax.numpy as jnp
import numpy as np
from jax import lax

P_SIZE = 8
ORD = 8
ORD_LOW = 2
CELL_DEV = 128
OWNERS = 8
HELPERS = 4
NCELL = 4096
REF_MAX = 64
GROUP_REF = 128


def draw_neighbours(key, part):
    blocks = NCELL // CELL_DEV
    device_ids = jnp.arange(blocks, dtype=jnp.int32)

    def shuffled(salt):
        subkeys = jax.random.split(jax.random.fold_in(key, salt), blocks)
        return jax.vmap(lambda subkey: jax.random.permutation(subkey, CELL_DEV))(subkeys).astype(jnp.int32)
    forward = shuffled(11)
    across_y = shuffled(12)
    across_z = shuffled(13)
    later = (device_ids + HELPERS) % blocks
    earlier = (device_ids - HELPERS) % blocks
    backward = jnp.argsort(forward, axis=1, stable=True).astype(jnp.int32)
    offsets = device_ids[:, None] * CELL_DEV
    plus_x = later[:, None] * CELL_DEV + forward
    minus_x = earlier[:, None] * CELL_DEV + backward[earlier]
    plus_y = offsets + across_y
    minus_y = offsets + jnp.argsort(across_y, axis=1, stable=True).astype(jnp.int32)
    plus_z = offsets + across_z
    minus_z = offsets + jnp.argsort(across_z, axis=1, stable=True).astype(jnp.int32)
    linked = jnp.stack([minus_x, plus_x, minus_y, plus_y, minus_z, plus_z])
    return linked.reshape(6, NCELL).astype(jnp.int32)


def block_levels(stream_key, shape, cuts, smallest, top_value):
    gain = 1.0
    for position, blocks in cuts:
        heights = jax.random.uniform(jax.random.fold_in(jax.random.fold_in(stream_key, 6), position), (blocks,), jnp.float32, smallest / len(cuts), top_value / len(cuts))
        gain = gain * jnp.repeat(jnp.exp(heights), shape[position] // blocks).reshape((-1,) + (1,) * (len(shape) - 1 - position))
    return gain


def split_up(amount, total, limit, lean):
    portions = [(1 << 20) // math.isqrt(standing ** lean) + 1 for standing in range(2, amount + 1)]
    rest, given = total - limit - (amount - 1), [1] * (amount - 1)
    while rest > 0:
        candidates = [i for i in range(amount - 1) if given[i] < limit]
        whole, budget = sum([portions[i] for i in candidates]), rest
        for i in candidates:
            extra = min(limit - given[i], max(1, budget * portions[i] // whole), rest)
            given[i] = given[i] + extra
            rest = rest - extra
    return np.array([limit] + given)


def uneven(rng, count, total, limit, lean):
    if count == 2:
        one = jax.random.randint(rng, (), max(1, total - limit), min(limit, total - 1) + 1)
        return jnp.stack([one, total - one])
    tallies = jnp.asarray(split_up(count, total, limit, lean), jnp.int32)
    pairs = (count - 1) // 2
    donor, receiver = tallies[1:1 + 2 * pairs:2], tallies[2:2 + 2 * pairs:2]
    slack = jnp.minimum(donor - 1, limit - receiver)
    moved = jax.random.randint(jax.random.fold_in(rng, 1), (pairs,), 0, 1 << 20) % (slack + 1)
    tallies = tallies.at[1:1 + 2 * pairs:2].set(donor - moved).at[2:2 + 2 * pairs:2].set(receiver + moved)
    return tallies[jax.random.permutation(jax.random.fold_in(rng, 2), count)]


def noise(key, extent, spread, limit, cuts=(), kind=jnp.bfloat16):
    entries = spread * jax.random.normal(key, extent, jnp.float32)
    if cuts:
        entries = entries * block_levels(key, extent, cuts, -0.22, 0.18)
    return jnp.clip(entries, -limit, limit).astype(kind)


def setup_inputs(seed: int = 0) -> dict:
    seeds = jax.random.split(jax.random.key(seed), 5)
    solution = noise(seeds[0], (9, NCELL, P_SIZE * P_SIZE * P_SIZE), 1.0, 6.0, ((1, 32),), jnp.float32)
    material = jnp.clip(0.5 + 1.5 * jax.random.uniform(seeds[1], (3, NCELL, P_SIZE * P_SIZE * P_SIZE), jnp.float32) ** block_levels(seeds[1], (3, NCELL, P_SIZE * P_SIZE * P_SIZE), ((1, 32),), -0.2, 0.2), 0.5, 2.0)
    neighbours = draw_neighbours(jax.random.fold_in(seeds[4], 71), 0)
    refine_count = jax.vmap(lambda own: uneven(own, HELPERS, GROUP_REF, REF_MAX, 2))(jax.random.split(seeds[3], OWNERS)).reshape((OWNERS, HELPERS)).astype(jnp.int32)
    return {"solution": solution, "material": material, "neighbours": neighbours, "refine_count": refine_count}


along_x = (6, 7, 8, 0, 3, 5)
along_y = (6, 7, 8, 3, 1, 4)
along_z = (6, 7, 8, 5, 4, 2)
time_step = 0.5
lift_gain = 0.5

def cheb_table(node_count):
    intervals = node_count - 1
    places = np.arange(node_count)
    points = np.cos(np.pi * places / intervals)
    weights = np.where((places == 0) | (places == intervals), 2.0, 1.0)
    scaled = weights * (-1.0) ** places
    differ = points[:, None] - points[None, :] + np.eye(node_count)
    matrix = np.outer(scaled, 1.0 / scaled) / differ
    matrix = matrix - np.eye(node_count) * np.sum(matrix, axis=1)[:, None]
    return matrix / (node_count * node_count / 4.0)

def taylor_weight(degree):
    return time_step ** (degree + 1) / math.factorial(degree + 1)

def derive(values, slope_table, direction):
    fields, cell_count = (values.shape[0], values.shape[1])
    volume = values.reshape(fields, cell_count, P_SIZE, P_SIZE, P_SIZE)
    pattern = ('ij,vcjbe->vcibe', 'ij,vcaje->vcaie', 'ij,vcabj->vcabi')[direction]
    result = jnp.einsum(pattern, slope_table, volume, precision=lax.Precision.HIGHEST)
    return result.reshape(fields, cell_count, P_SIZE * P_SIZE * P_SIZE)

def elastic(slope_x, slope_y, slope_z, material):
    density, lame_first, shear_modulus = (material[0], material[1], material[2])
    diverge = slope_x[0] + slope_y[1] + slope_z[2]
    normal_x = lame_first * diverge + 2.0 * shear_modulus * slope_x[0]
    normal_y = lame_first * diverge + 2.0 * shear_modulus * slope_y[1]
    normal_z = lame_first * diverge + 2.0 * shear_modulus * slope_z[2]
    shear_xy = shear_modulus * (slope_y[0] + slope_x[1])
    shear_yz = shear_modulus * (slope_z[1] + slope_y[2])
    shear_xz = shear_modulus * (slope_z[0] + slope_x[2])
    speed_x = (slope_x[3] + slope_y[3] + slope_z[3]) / density
    speed_y = (slope_x[4] + slope_y[4] + slope_z[4]) / density
    speed_z = (slope_x[5] + slope_y[5] + slope_z[5]) / density
    return jnp.stack([normal_x, normal_y, normal_z, shear_xy, shear_yz, shear_xz, speed_x, speed_y, speed_z])

def operate(values, material, slope_table):
    picks = (along_x, along_y, along_z)
    slopes = [derive(jnp.stack([values[member] for member in picks[direction]]), slope_table, direction) for direction in range(3)]
    return elastic(slopes[0], slopes[1], slopes[2], material)

def face_trace(values, direction, place):
    fields, cell_count = (values.shape[0], values.shape[1])
    volume = values.reshape(fields, cell_count, P_SIZE, P_SIZE, P_SIZE)
    chosen = (slice(None), slice(None)) + (slice(None),) * direction + (place,)
    return volume[chosen].reshape(fields, cell_count, P_SIZE * P_SIZE)

def add_trace(volume, correction, direction, place):
    fields, cell_count = (volume.shape[0], volume.shape[1])
    chosen = (slice(None), slice(None)) + (slice(None),) * direction + (place,)
    return volume.at[chosen].add(correction.reshape(fields, cell_count, P_SIZE, P_SIZE))

def face_flux(own_trace, far_trace, own_speed, far_speed, medium, direction, normal_sign):
    picks = (along_x, along_y, along_z)
    difference = far_trace - own_trace
    top_speed = jnp.maximum(own_speed, far_speed)
    nothing = (0.0,) * 6
    slopes = [nothing, nothing, nothing]
    slopes[direction] = tuple((difference[member] for member in picks[direction]))
    normal = elastic(slopes[0], slopes[1], slopes[2], medium)
    return lift_gain * (0.5 * normal_sign * normal + 0.5 * top_speed[None] * difference)

def continue_terms(current, material, slope_table):
    extra_part = jnp.zeros_like(current)
    for degree in range(ORD_LOW, ORD):
        current = operate(current, material, slope_table)
        extra_part = extra_part + taylor_weight(degree) * current
    return extra_part

def predict(solution, material, slope_table):
    current = solution
    base_part = time_step * solution
    for degree in range(1, ORD_LOW):
        current = operate(current, material, slope_table)
        base_part = base_part + taylor_weight(degree) * current
    return (base_part, continue_terms(current, material, slope_table))

def reference(solution, material, neighbours, refine_count):
    slope_table = jnp.asarray(cheb_table(P_SIZE), jnp.float32)
    blocks = solution.shape[1] // CELL_DEV
    counts = refine_count.reshape(-1)
    local_ids = jnp.arange(CELL_DEV, dtype=jnp.int32)

    def predict_block(block_index, buffer):
        offset = (block_index * CELL_DEV).astype(jnp.int32)
        values = lax.dynamic_slice_in_dim(solution, offset, CELL_DEV, 1)
        medium = lax.dynamic_slice_in_dim(material, offset, CELL_DEV, 1)
        refined_limit = lax.dynamic_index_in_dim(counts, block_index.astype(jnp.int32), 0, keepdims=False)
        base_part, extra_part = predict(values, medium, slope_table)
        refined = local_ids < refined_limit
        combined = base_part + jnp.where(refined[None, :, None], extra_part, 0.0)
        return lax.dynamic_update_slice_in_dim(buffer, combined, offset, 1)
    integral = lax.fori_loop(0, blocks, predict_block, jnp.zeros_like(solution))
    wave_speed = jnp.sqrt((material[1] + 2.0 * material[2]) / material[0])

    def correct_block(block_index, buffer):
        offset = (block_index * CELL_DEV).astype(jnp.int32)
        values = lax.dynamic_slice_in_dim(integral, offset, CELL_DEV, 1)
        medium = lax.dynamic_slice_in_dim(material, offset, CELL_DEV, 1)
        start_state = lax.dynamic_slice_in_dim(solution, offset, CELL_DEV, 1)
        neighbour_ids = lax.dynamic_slice_in_dim(neighbours, offset, CELL_DEV, 1)
        speeds = lax.dynamic_slice_in_dim(wave_speed, offset, CELL_DEV, 0)
        result = start_state + operate(values, medium, slope_table)
        volume = result.reshape(9, CELL_DEV, P_SIZE, P_SIZE, P_SIZE)
        for face_id in range(6):
            direction = face_id // 2
            upper_side = face_id % 2 == 1
            own_place = 0 if upper_side else P_SIZE - 1
            far_place = P_SIZE - 1 if upper_side else 0
            normal_sign = 1.0 if upper_side else -1.0
            partner = jnp.take(integral, neighbour_ids[face_id], axis=1)
            partner_speed = jnp.take(wave_speed, neighbour_ids[face_id], axis=0)
            correction = face_flux(face_trace(values, direction, own_place), face_trace(partner, direction, far_place), face_trace(speeds[None], direction, own_place)[0], face_trace(partner_speed[None], direction, far_place)[0], face_trace(medium, direction, own_place), direction, normal_sign)
            volume = add_trace(volume, correction, direction, own_place)
        return lax.dynamic_update_slice_in_dim(buffer, volume.reshape(9, CELL_DEV, P_SIZE * P_SIZE * P_SIZE), offset, 1)
    return lax.fori_loop(0, blocks, correct_block, jnp.zeros_like(solution))
```

```python
import math

import jax
import jax.numpy as jnp
import ml_dtypes
import numpy as np
from jax import lax
from jax.experimental import pallas as pl
from jax.experimental.pallas import tpu as pltpu
from jax.sharding import PartitionSpec as P

P_SIZE = 8
ORD = 8
REF_MAX = 64
LANES = 128
TILES = 4
HALF = 64
SUB = 8

along_x = (6, 7, 8, 0, 3, 5)
along_y = (6, 7, 8, 3, 1, 4)
along_z = (6, 7, 8, 5, 4, 2)
both_yz = (6, 7, 8, 4)
pairs_yz = ((1, 2), (3, 5))
time_step = 0.5
VMEM_LIMIT = 56 * 1024 * 1024


def cheb_table(node_count):
    intervals = node_count - 1
    places = np.arange(node_count)
    points = np.cos(np.pi * places / intervals)
    weights = np.where((places == 0) | (places == intervals), 2.0, 1.0)
    scaled = weights * (-1.0) ** places
    differ = points[:, None] - points[None, :] + np.eye(node_count)
    matrix = np.outer(scaled, 1.0 / scaled) / differ
    matrix = matrix - np.eye(node_count) * np.sum(matrix, axis=1)[:, None]
    return matrix / (node_count * node_count / 4.0)


def taylor_weight(degree):
    return time_step ** (degree + 1) / math.factorial(degree + 1)


def tables():
    slope = cheb_table(P_SIZE).astype(np.float32).astype(np.float64)
    high = slope.astype(ml_dtypes.bfloat16).astype(np.float64)
    low = slope - high
    one = np.eye(P_SIZE)
    two = np.eye(2)

    def spread(matrix):
        along_b = np.kron(two, np.kron(matrix.T, one))
        along_e = np.kron(two, np.kron(one, matrix.T))
        return along_b, along_e

    hy, hz = spread(high)
    ly, lz = spread(low)
    none = np.zeros_like(hy)
    w1 = np.concatenate(
        [np.concatenate([hy, hz], 1), np.concatenate([hy, hz], 1), np.concatenate([ly, lz], 1)], 0
    )
    diag_high = np.block([[hy, none], [none, hz]])
    diag_low = np.block([[ly, none], [none, lz]])
    w2 = np.concatenate([diag_high, diag_high, diag_low], 0)

    half = P_SIZE // 2
    top = slope[:half, :half]
    mirror = slope[:half, ::-1][:, :half]
    parts = ((top + mirror) / 2, (top - mirror) / 2)
    lane_half = np.arange(LANES) // HALF
    rows = []
    for part in parts:
        for t in range(2):
            for s in range(2):
                for swap in range(2):
                    source = lane_half if swap == 0 else 1 - lane_half
                    rows.append(part[2 * t + lane_half, 2 * s + source])
    xc = np.broadcast_to(np.stack(rows)[:, None, :], (len(rows), SUB, LANES))
    return (
        jnp.asarray(w1.astype(ml_dtypes.bfloat16)),
        jnp.asarray(w2.astype(ml_dtypes.bfloat16)),
        jnp.asarray(np.ascontiguousarray(xc).astype(np.float32)),
    )


def roll(value, by):
    by = by % LANES
    return value if by == 0 else pltpu.roll(value, by, value.ndim - 1)


def lane_ids(rows):
    return lax.broadcasted_iota(jnp.int32, (rows, LANES), 1)


def split(value):
    high = value.astype(jnp.bfloat16)
    return high, (value - high.astype(jnp.float32)).astype(jnp.bfloat16)


def x_slope(parts, xc_ref):
    mirrored = [roll(parts[3 - t], HALF) for t in range(2)]
    even = [parts[t] + mirrored[t] for t in range(2)]
    odd = [parts[t] - mirrored[t] for t in range(2)]
    sources = [[even, [roll(v, HALF) for v in even]], [odd, [roll(v, HALF) for v in odd]]]
    result = [None] * TILES
    for t in range(2):
        sums = []
        for kind in range(2):
            total = None
            for s in range(2):
                for swap in range(2):
                    term = sources[kind][swap][s] * xc_ref[((kind * 2 + t) * 2 + s) * 2 + swap]
                    total = term if total is None else total + term
            sums.append(total)
        result[t] = sums[0] + sums[1]
        result[3 - t] = roll(sums[1] - sums[0], HALF)
    return result


def apply_operator(load, material, tabs, scratch, rows, scale, emit):
    w1_ref, w2_ref, xc_ref = tabs
    a1, a2, o1, o2 = scratch
    for i, f in enumerate(both_yz):
        for t in range(TILES):
            high, low = split(load(f, 0, rows, t))
            at = pl.ds((i * TILES + t) * rows, rows)
            a1[at, 0:LANES] = high
            a1[at, LANES : 2 * LANES] = low
            a1[at, 2 * LANES : 3 * LANES] = high
    for i, pair in enumerate(pairs_yz):
        for t in range(TILES):
            at = pl.ds((i * TILES + t) * rows, rows)
            for place, f in enumerate(pair):
                high, low = split(load(f, 0, rows, t))
                for block, piece in ((0, high), (2, low), (4, high)):
                    column = (block + place) * LANES
                    a2[at, column : column + LANES] = piece
    o1[...] = jnp.dot(a1[...], w1_ref[...], preferred_element_type=jnp.float32)
    o2[...] = jnp.dot(a2[...], w2_ref[...], preferred_element_type=jnp.float32)

    def yz(ref, i, t, r):
        at = pl.ds((i * TILES + t) * rows + r, SUB)
        return ref[at, 0:LANES], ref[at, LANES : 2 * LANES]

    for r in range(0, rows, SUB):
        slopes = {f: x_slope([load(f, r, SUB, t) for t in range(TILES)], xc_ref) for f in along_x}
        factor = scale(r)
        for t in range(TILES):
            lame, shear, light = [
                m if factor is None else m * factor for m in material(r, t)
            ]
            shear_2 = shear + shear
            dy_vx, dz_vx = yz(o1, 0, t, r)
            dy_vy, dz_vy = yz(o1, 1, t, r)
            dy_vz, dz_vz = yz(o1, 2, t, r)
            dy_syz, dz_syz = yz(o1, 3, t, r)
            dy_syy, dz_szz = yz(o2, 0, t, r)
            dy_sxy, dz_sxz = yz(o2, 1, t, r)
            dx_vx, dx_vy, dx_vz = (slopes[f][t] for f in (6, 7, 8))
            diverge = lame * (dx_vx + dy_vy + dz_vz)
            emit(0, r, t, diverge + shear_2 * dx_vx)
            emit(1, r, t, diverge + shear_2 * dy_vy)
            emit(2, r, t, diverge + shear_2 * dz_vz)
            emit(3, r, t, shear * (dy_vx + dx_vy))
            emit(4, r, t, shear * (dz_vy + dy_vz))
            emit(5, r, t, shear * (dz_vx + dx_vz))
            emit(6, r, t, light * (slopes[0][t] + dy_sxy + dz_sxz))
            emit(7, r, t, light * (slopes[3][t] + dy_syy + dz_syz))
            emit(8, r, t, light * (slopes[5][t] + dy_syz + dz_szz))


def span(tile):
    return slice(tile * LANES, (tile + 1) * LANES)


def pack_faces(read, rows):
    low = lane_ids(rows // 2) < HALF
    first, second = read(0, 0), read(rows // 2, 0)
    start = jnp.where(low, first, roll(second, HALF))
    first, second = read(0, 3), read(rows // 2, 3)
    end = jnp.where(low, roll(first, HALF), second)
    return end, start


def wave_speed(density, lame, shear):
    return jnp.sqrt((lame + 2.0 * shear) / density)


def early_kernel(sol_ref, mat_ref, edge_ref, w1_ref, w2_ref, xc_ref, out_ref, end_ref, start_ref, a1, a2, o1, o2):
    rows = sol_ref.shape[1]
    load = lambda f, r, count, t: sol_ref[f, r : r + count, span(t)]
    material = lambda r, t: (
        mat_ref[1, r : r + SUB, span(t)],
        mat_ref[2, r : r + SUB, span(t)],
        1.0 / mat_ref[0, r : r + SUB, span(t)],
    )

    def emit(f, r, t, value):
        base = time_step * sol_ref[f, r : r + SUB, span(t)]
        out_ref[f, r : r + SUB, span(t)] = base + value

    apply_operator(
        load, material, (w1_ref, w2_ref, xc_ref), (a1, a2, o1, o2), rows, lambda r: taylor_weight(1), emit
    )
    count = rows // 2
    for f in range(9):
        end, start = pack_faces(lambda r, t, f=f: out_ref[f, r : r + count, span(t)], rows)
        end_ref[f] = end
        start_ref[f] = start
    for i, ref in enumerate((edge_ref, mat_ref)):

        def speed(r, t, ref=ref):
            return wave_speed(*[ref[m, r : r + count, span(t)] for m in range(3)])

        end, start = pack_faces(speed, rows)
        end_ref[9 + i] = end
        start_ref[9 + i] = start


def refined_kernel(count_ref, sol_ref, mat_ref, w1_ref, w2_ref, xc_ref, out_ref, end_ref, start_ref, state, light, a1, a2, o1, o2):
    rows = sol_ref.shape[1]
    limit = count_ref[0, 0]
    for f in range(9):
        first = time_step * sol_ref[f]
        state[f] = first
        out_ref[f] = first
    light[...] = 1.0 / mat_ref[0]
    load = lambda f, r, count, t: state[f, r : r + count, span(t)]
    material = lambda r, t: (
        mat_ref[1, r : r + SUB, span(t)],
        mat_ref[2, r : r + SUB, span(t)],
        light[r : r + SUB, span(t)],
    )

    def emit(f, r, t, value):
        state[f, r : r + SUB, span(t)] = value
        out_ref[f, r : r + SUB, span(t)] = out_ref[f, r : r + SUB, span(t)] + value

    def term(degree, carry):
        ratio = time_step / jnp.full((SUB, LANES), degree + 1, jnp.int32).astype(jnp.float32)
        bound = jnp.where(degree < 2, rows, limit)

        def scale(r):
            ids = r + lax.broadcasted_iota(jnp.int32, (SUB, LANES), 0)
            return jnp.where(ids < bound, ratio, 0.0)

        apply_operator(load, material, (w1_ref, w2_ref, xc_ref), (a1, a2, o1, o2), rows, scale, emit)
        return carry

    lax.fori_loop(1, ORD, term, 0)
    count = rows // 2
    for f in range(9):
        end, start = pack_faces(lambda r, t, f=f: out_ref[f, r : r + count, span(t)], rows)
        end_ref[f] = end
        start_ref[f] = start


def hot(row, first, count):
    cells = row.shape[1]
    ids = first + lax.broadcasted_iota(jnp.int32, (count, cells), 0)
    return jnp.where(ids == row, 1.0, 0.0).T


def unpack_faces(after, before):
    low = lane_ids(after.shape[0]) < HALF
    return jnp.concatenate(
        [
            jnp.where(low, after, 0.0),
            jnp.where(low, roll(after, HALF), 0.0),
            jnp.where(low, 0.0, roll(before, HALF)),
            jnp.where(low, 0.0, before),
        ],
        0,
    )


def flux(direction, jump, far_less, lame, shear, light, speed, sign):
    members = ((6, 7, 8, 0, 3, 5), (6, 7, 8, 3, 1, 4), (6, 7, 8, 5, 4, 2))[direction]
    g = [jump[m] for m in members]
    through = g[direction]
    spread_out = lame * through
    normal = [spread_out, spread_out, spread_out, None, None, None, light * g[3], light * g[4], light * g[5]]
    normal[direction] = spread_out + 2.0 * (shear * through)
    if direction == 0:
        normal[3], normal[5] = shear * g[1], shear * g[2]
    elif direction == 1:
        normal[3], normal[4] = shear * g[0], shear * g[2]
    else:
        normal[4], normal[5] = shear * g[1], shear * g[0]
    return [
        speed * jump[f] if normal[f] is None else normal[f] + speed * jump[f] for f in range(9)
    ]


def correct_kernel(
    sol_ref, mat_ref, low_ref, high_ref, near_ref, after_ref, before_ref, w1_ref, w2_ref, xc_ref,
    out_ref, xmat_ref, late_ref, a1, a2, o1, o2, compact, hot_ref, rhs, far, fix, light,
):
    cells = sol_ref.shape[1]
    half = low_ref.shape[1]
    lanes = lane_ids(SUB)
    light[...] = 1.0 / mat_ref[0]

    def integral(f, r, count, t):
        if r < half:
            return low_ref[f, r : r + count, span(t)]
        return high_ref[f, r - half : r - half + count, span(t)]

    step = (0, 16, 2)
    shift = (0, 56, 7)
    in_y = (lanes % HALF < 8) | (lanes % HALF >= 56)
    in_z = (lanes % 8 == 0) | (lanes % 8 == 7)
    starts = (lanes < HALF, lanes % HALF < 0, lanes % 8 < 0)

    def squeeze(read, direction):
        if direction == 0:
            return jnp.where(lanes < HALF, read(0), read(3))
        inside = (None, in_y, in_z)[direction]
        total = read(0)
        for t in range(1, TILES):
            mask = owner[direction] == t
            total = jnp.where(mask, roll(read(t), step[direction] * t), total)
        return total

    owner = (None, ((lanes + 72) % HALF) // 16, ((lanes + 1) % 8) // 2)
    y_home = (lanes - 16 * owner[1] + LANES) % LANES
    z_home = (lanes - 2 * owner[2] + LANES) % LANES
    first = (lanes < HALF, y_home % HALF < 8, z_home % 8 == 0)

    for direction in range(3):
        for r in range(0, cells, SUB):
            at = pl.ds(r, SUB)
            for f in range(9):
                compact[direction, f, at, :] = squeeze(lambda t: integral(f, r, SUB, t), direction)
            density = squeeze(lambda t: mat_ref[0, at, span(t)], direction)
            lame = squeeze(lambda t: mat_ref[1, at, span(t)], direction)
            shear = squeeze(lambda t: mat_ref[2, at, span(t)], direction)
            side = jnp.where(first[direction], 0.25, -0.25)
            compact[direction, 9, at, :] = wave_speed(density, lame, shear)
            compact[direction, 10, at, :] = side * lame
            compact[direction, 11, at, :] = side * shear
            compact[direction, 12, at, :] = side / density

    here = near_ref[...] % cells
    for direction in (1, 2):
        plus = hot(here[2 * direction + 1 : 2 * direction + 2], 0, cells).astype(jnp.bfloat16)
        minus = hot(here[2 * direction : 2 * direction + 1], 0, cells).astype(jnp.bfloat16)
        for k in range(2):
            hot_ref[:, 2 * k * LANES : (2 * k + 1) * LANES] = plus
            hot_ref[:, (2 * k + 1) * LANES : (2 * k + 2) * LANES] = minus
        starting = jnp.broadcast_to(first[direction][0:1], (cells, LANES))
        for f in range(10):
            own = compact[direction, f]
            up = jnp.where(starting, roll(own, -shift[direction]), 0.0)
            down = jnp.where(starting, 0.0, roll(own, shift[direction]))
            for k, piece in enumerate((up, down)):
                high, low = split(piece)
                rhs[k * LANES : (k + 1) * LANES, span(f)] = high
                rhs[(k + 2) * LANES : (k + 3) * LANES, span(f)] = low
        far[...] = jnp.dot(hot_ref[...], rhs[...], preferred_element_type=jnp.float32)
        for r in range(0, cells, SUB):
            at = pl.ds(r, SUB)
            jump = [far[at, span(f)] - compact[direction, f, at, :] for f in range(9)]
            speed = 0.25 * jnp.maximum(far[at, span(9)], compact[direction, 9, at, :])
            lame, shear, weight = (compact[direction, i, at, :] for i in (10, 11, 12))
            for f, value in enumerate(flux(direction, jump, None, lame, shear, weight, speed, None)):
                fix[direction, f, at, :] = value

    plus = here[1:2]
    minus = here[0:1]
    pieces = [hot(plus, half, half), hot(minus, half, half), hot(plus, 0, half), hot(minus, 0, half)]
    early = jnp.concatenate(pieces[:2], 1).astype(jnp.bfloat16)
    late = jnp.concatenate(pieces[2:], 1).astype(jnp.bfloat16)
    late_ref[:, :LANES] = late
    late_ref[:, LANES:] = late
    hot_ref[:, 0 * LANES : 1 * LANES] = early
    hot_ref[:, 1 * LANES : 2 * LANES] = early
    hot_ref[:, 2 * LANES : 3 * LANES] = late
    hot_ref[:, 3 * LANES : 4 * LANES] = late
    for f in range(9):
        high, low = split(unpack_faces(after_ref[f], before_ref[f]))
        rhs[0:LANES, span(f)] = high
        rhs[LANES : 2 * LANES, span(f)] = low
    for k, f in ((0, 10), (2, 9)):
        high, low = split(unpack_faces(after_ref[f], before_ref[f]))
        rhs[k * LANES : (k + 1) * LANES, span(9)] = high
        rhs[(k + 1) * LANES : (k + 2) * LANES, span(9)] = low
    far[:, : 9 * LANES] = jnp.dot(
        hot_ref[:, : 2 * LANES], rhs[: 2 * LANES, : 9 * LANES], preferred_element_type=jnp.float32
    )
    far[:, span(9)] = jnp.dot(hot_ref[...], rhs[:, span(9)], preferred_element_type=jnp.float32)
    for r in range(0, cells, SUB):
        at = pl.ds(r, SUB)
        jump = [far[at, span(f)] - compact[0, f, at, :] for f in range(9)]
        speed = 0.25 * jnp.maximum(far[at, span(9)], compact[0, 9, at, :])
        lame, shear, weight = (compact[0, i, at, :] for i in (10, 11, 12))
        for f, value in enumerate(flux(0, jump, None, lame, shear, weight, speed, None)):
            fix[0, f, at, :] = value
        for i, value in enumerate((lame, shear, weight, speed)):
            xmat_ref[i, at, :] = value

    for start in range(0, cells, half):
        load = lambda f, r, count, t: integral(f, start + r, count, t)
        material = lambda r, t: (
            mat_ref[1, start + r : start + r + SUB, span(t)],
            mat_ref[2, start + r : start + r + SUB, span(t)],
            light[start + r : start + r + SUB, span(t)],
        )

        def emit(f, r, t, value):
            at = pl.ds(start + r, SUB)
            total = sol_ref[f, at, span(t)] + value
            total = total + jnp.where(in_y, roll(fix[1, f, at, :], -step[1] * t), 0.0)
            total = total + jnp.where(in_z, roll(fix[2, f, at, :], -step[2] * t), 0.0)
            if t == 0:
                total = total + jnp.where(lanes < HALF, fix[0, f, at, :], 0.0)
            if t == TILES - 1:
                total = total + jnp.where(lanes < HALF, 0.0, fix[0, f, at, :])
            out_ref[f, at, span(t)] = total

        apply_operator(
            load, material, (w1_ref, w2_ref, xc_ref), (a1, a2, o1, o2), half, lambda r: None, emit
        )


def finish_kernel(done_ref, after_ref, before_ref, xmat_ref, late_ref, out_ref, ends, rhs, far, sems):
    cells = ends.shape[2]
    places = (0, TILES - 1)
    loads = [
        pltpu.make_async_copy(done_ref.at[:, :, pl.ds(t * LANES, LANES)], ends.at[i], sems.at[i])
        for i, t in enumerate(places)
    ]
    for copy in loads:
        copy.start()
    for f in range(9):
        high, low = split(unpack_faces(after_ref[f], before_ref[f]))
        rhs[0:LANES, span(f)] = high
        rhs[LANES : 2 * LANES, span(f)] = low
    far[...] = jnp.dot(late_ref[...], rhs[...], preferred_element_type=jnp.float32)
    for copy in loads:
        copy.wait()
    low_half = lane_ids(SUB) < HALF
    for r in range(0, cells, SUB):
        at = pl.ds(r, SUB)
        jump = [far[at, span(f)] for f in range(9)]
        lame, shear, weight, speed = (xmat_ref[i, at, :] for i in range(4))
        for f, value in enumerate(flux(0, jump, None, lame, shear, weight, speed, None)):
            ends[0, f, at, :] = ends[0, f, at, :] + jnp.where(low_half, value, 0.0)
            ends[1, f, at, :] = ends[1, f, at, :] + jnp.where(low_half, 0.0, value)
    stores = [
        pltpu.make_async_copy(ends.at[i], out_ref.at[:, :, pl.ds(t * LANES, LANES)], sems.at[i])
        for i, t in enumerate(places)
    ]
    for copy in stores:
        copy.start()
    for copy in stores:
        copy.wait()


def shifted(value, axis, by):
    peers = lax.axis_size(axis)
    return lax.ppermute(value, axis, [(i, (i + by) % peers) for i in range(peers)])


def block(shape, *place):
    return pl.BlockSpec(shape, lambda i: place)


def whole(shape):
    return pl.BlockSpec(shape, lambda i: (0,) * len(shape))


def f32(*shape):
    return jax.ShapeDtypeStruct(shape, jnp.float32)


def operator_scratch(rows):
    return [
        pltpu.VMEM((len(both_yz) * TILES * rows, 3 * LANES), jnp.bfloat16),
        pltpu.VMEM((len(pairs_yz) * TILES * rows, 6 * LANES), jnp.bfloat16),
        pltpu.VMEM((len(both_yz) * TILES * rows, 2 * LANES), jnp.float32),
        pltpu.VMEM((len(pairs_yz) * TILES * rows, 2 * LANES), jnp.float32),
    ]


def on_device(solution, material, neighbours, refine_count):
    cells, nodes = solution.shape[1:]
    rows = REF_MAX
    w1, w2, xc = tables()
    params = pltpu.CompilerParams(vmem_limit_bytes=VMEM_LIMIT)
    table_specs = [whole(w1.shape), whole(w2.shape), whole(xc.shape)]
    early_shape, late_shape = (11, rows // 2, LANES), (9, rows // 2, LANES)

    high, end, start = pl.pallas_call(
        early_kernel,
        grid=(1,),
        in_specs=[
            block((9, rows, nodes), 0, 1, 0),
            block((3, rows, nodes), 0, 1, 0),
            block((3, rows, nodes), 0, 0, 0),
        ]
        + table_specs,
        out_specs=[whole((9, rows, nodes)), whole(early_shape), whole(early_shape)],
        out_shape=[f32(9, rows, nodes), f32(*early_shape), f32(*early_shape)],
        scratch_shapes=operator_scratch(rows),
        compiler_params=params,
        name="early",
    )(solution, material, material, w1, w2, xc)
    early_after = shifted(end, "space", -1)
    early_before = shifted(start, "space", 1)

    low, end, start = pl.pallas_call(
        refined_kernel,
        grid=(1,),
        in_specs=[
            pl.BlockSpec(memory_space=pltpu.SMEM),
            block((9, rows, nodes), 0, 0, 0),
            block((3, rows, nodes), 0, 0, 0),
        ]
        + table_specs,
        out_specs=[whole((9, rows, nodes)), whole(late_shape), whole(late_shape)],
        out_shape=[f32(9, rows, nodes), f32(*late_shape), f32(*late_shape)],
        scratch_shapes=[
            pltpu.VMEM((9, rows, nodes), jnp.float32),
            pltpu.VMEM((rows, nodes), jnp.float32),
        ]
        + operator_scratch(rows),
        compiler_params=params,
        name="refined",
    )(refine_count, solution, material, w1, w2, xc)
    late_after = shifted(end, "space", -1)
    late_before = shifted(start, "space", 1)

    done, xmat, late_hot = pl.pallas_call(
        correct_kernel,
        grid=(1,),
        in_specs=[
            whole(solution.shape),
            whole(material.shape),
            whole(low.shape),
            whole(high.shape),
            whole(neighbours.shape),
            whole(early_shape),
            whole(early_shape),
        ]
        + table_specs,
        out_specs=[whole(solution.shape), whole((4, cells, LANES)), whole((cells, 2 * LANES))],
        out_shape=[
            f32(*solution.shape),
            f32(4, cells, LANES),
            jax.ShapeDtypeStruct((cells, 2 * LANES), jnp.bfloat16),
        ],
        scratch_shapes=operator_scratch(rows)
        + [
            pltpu.VMEM((3, 13, cells, LANES), jnp.float32),
            pltpu.VMEM((cells, 4 * LANES), jnp.bfloat16),
            pltpu.VMEM((4 * LANES, 10 * LANES), jnp.bfloat16),
            pltpu.VMEM((cells, 10 * LANES), jnp.float32),
            pltpu.VMEM((3, 9, cells, LANES), jnp.float32),
            pltpu.VMEM((cells, nodes), jnp.float32),
        ],
        compiler_params=params,
        name="correct",
    )(solution, material, low, high, neighbours, early_after, early_before, w1, w2, xc)

    return pl.pallas_call(
        finish_kernel,
        grid=(1,),
        in_specs=[
            pl.BlockSpec(memory_space=pl.ANY),
            whole(late_shape),
            whole(late_shape),
            whole(xmat.shape),
            whole(late_hot.shape),
        ],
        out_specs=pl.BlockSpec(memory_space=pl.ANY),
        out_shape=f32(*solution.shape),
        scratch_shapes=[
            pltpu.VMEM((2, 9, cells, LANES), jnp.float32),
            pltpu.VMEM((2 * LANES, 9 * LANES), jnp.bfloat16),
            pltpu.VMEM((cells, 9 * LANES), jnp.float32),
            pltpu.SemaphoreType.DMA((2,)),
        ],
        input_output_aliases={0: 0},
        compiler_params=params,
        name="finish",
    )(done, late_after, late_before, xmat, late_hot)


def solution(mesh):
    in_specs = (
        P(None, ("space", "help"), None),
        P(None, ("space", "help"), None),
        P(None, ("space", "help")),
        P("space", "help"),
    )
    out_specs = P(None, ("space", "help"), None)
    return jax.shard_map(
        on_device, mesh=mesh, in_specs=in_specs, out_specs=out_specs, check_vma=False
    )
```

```python
import math

import jax
import jax.numpy as jnp
import ml_dtypes
import numpy as np
from jax import lax
from jax.experimental import pallas as pl
from jax.experimental.pallas import tpu as pltpu
from jax.sharding import PartitionSpec as P

P_SIZE = 8
ORD = 8
REF_MAX = 64
LANES = 128
TILES = 4
HALF = 64
SUB = 8
OPERATOR_SCRATCH = 6
LOADED = 7

along_x = (6, 7, 8, 0, 3, 5)
along_y = (6, 7, 8, 3, 1, 4)
along_z = (6, 7, 8, 5, 4, 2)
both_yz = (6, 7, 8, 4)
pairs_yz = ((1, 2), (3, 5))
time_step = 0.5


def cheb_table(node_count):
    intervals = node_count - 1
    places = np.arange(node_count)
    points = np.cos(np.pi * places / intervals)
    weights = np.where((places == 0) | (places == intervals), 2.0, 1.0)
    scaled = weights * (-1.0) ** places
    differ = points[:, None] - points[None, :] + np.eye(node_count)
    matrix = np.outer(scaled, 1.0 / scaled) / differ
    matrix = matrix - np.eye(node_count) * np.sum(matrix, axis=1)[:, None]
    return matrix / (node_count * node_count / 4.0)


def taylor_weight(degree):
    return time_step ** (degree + 1) / math.factorial(degree + 1)


def tables():
    slope = cheb_table(P_SIZE).astype(np.float32).astype(np.float64)
    high = slope.astype(ml_dtypes.bfloat16).astype(np.float64)
    low = slope - high
    one = np.eye(P_SIZE)
    two = np.eye(2)

    def spread(matrix):
        along_b = np.kron(two, np.kron(matrix.T, one))
        along_e = np.kron(two, np.kron(one, matrix.T))
        return along_b, along_e

    hy, hz = spread(high)
    ly, lz = spread(low)
    none = np.zeros_like(hy)
    w1 = np.concatenate(
        [np.concatenate([hy, hz], 1), np.concatenate([hy, hz], 1), np.concatenate([ly, lz], 1)], 0
    )
    diag_high = np.block([[hy, none], [none, hz]])
    diag_low = np.block([[ly, none], [none, lz]])
    w2 = np.concatenate([diag_high, diag_high, diag_low], 0)

    lane_half = np.arange(LANES) // HALF
    rows = []
    for t in range(TILES):
        for s in range(TILES):
            for source in (lane_half, 1 - lane_half):
                rows.append(slope[2 * t + lane_half, 2 * s + source])
    xc = np.broadcast_to(np.stack(rows)[:, None, :], (len(rows), SUB, LANES))
    return (
        jnp.asarray(w1.astype(ml_dtypes.bfloat16)),
        jnp.asarray(w2.astype(ml_dtypes.bfloat16)),
        jnp.asarray(np.ascontiguousarray(xc).astype(np.float32)),
    )


def face_tables():
    node = np.arange(P_SIZE**3)
    places = (node // P_SIZE % P_SIZE, node % P_SIZE)
    others = (node // HALF * P_SIZE + node % P_SIZE, node // P_SIZE)
    pick = np.zeros((P_SIZE**3, 2 * LANES))
    for k in range(2):
        for side, place in enumerate((0, P_SIZE - 1)):
            on = places[k] == place
            pick[node[on], k * LANES + side * HALF + others[k][on]] = 1.0
    squeeze = np.concatenate([pick, pick], 0).astype(ml_dtypes.bfloat16)
    spread = np.concatenate([pick.T, pick.T], 0).astype(ml_dtypes.bfloat16)
    return jnp.asarray(squeeze), jnp.asarray(spread)


def roll(value, by):
    by = by % LANES
    return value if by == 0 else pltpu.roll(value, by, value.ndim - 1)


def lane_ids(rows):
    return lax.broadcasted_iota(jnp.int32, (rows, LANES), 1)


def split(value):
    high = value.astype(jnp.bfloat16)
    return high, (value - high.astype(jnp.float32)).astype(jnp.bfloat16)


def x_slopes(load, turned, rows, slopes, xc_ref):
    for i, f in enumerate(along_x):
        for t in range(TILES):
            turned[i, :, span(t)] = roll(load(f, 0, rows, t), HALF)
    for i, f in enumerate(along_x):
        for r in range(0, rows, SUB):
            at = pl.ds(r, SUB)
            own = [load(f, r, SUB, t) for t in range(TILES)]
            other = [turned[i, at, span(t)] for t in range(TILES)]
            for t in range(TILES):
                total = None
                for s in range(TILES):
                    for swap, source in enumerate((own[s], other[s])):
                        term = source * xc_ref[(t * TILES + s) * 2 + swap]
                        total = term if total is None else total + term
                slopes[i, at, span(t)] = total


def begin_operator(load, parts, tabs, scratch, rows):
    w1_ref, w2_ref, xc_ref = tabs
    a1, a2, o1, o2, turned, slopes = scratch
    for i, f in enumerate(both_yz):
        for t in range(TILES):
            high, low = parts(f, t)
            at = pl.ds((i * TILES + t) * rows, rows)
            a1[at, 0:LANES] = high
            a1[at, LANES : 2 * LANES] = low
            a1[at, 2 * LANES : 3 * LANES] = high
    for i, pair in enumerate(pairs_yz):
        for t in range(TILES):
            at = pl.ds((i * TILES + t) * rows, rows)
            for place, f in enumerate(pair):
                high, low = parts(f, t)
                for block, piece in ((0, high), (2, low), (4, high)):
                    column = (block + place) * LANES
                    a2[at, column : column + LANES] = piece
    o1[...] = jnp.dot(a1[...], w1_ref[...], preferred_element_type=jnp.float32)
    o2[...] = jnp.dot(a2[...], w2_ref[...], preferred_element_type=jnp.float32)
    x_slopes(load, turned, rows, slopes, xc_ref)


def end_operator(material, scratch, rows, scale, emit):
    _, _, o1, o2, _, slopes = scratch

    def yz(ref, i, t, r):
        at = pl.ds((i * TILES + t) * rows + r, SUB)
        return ref[at, 0:LANES], ref[at, LANES : 2 * LANES]

    for r in range(0, rows, SUB):
        factor = scale(r)
        for t in range(TILES):
            lame, shear, light = [m if factor is None else m * factor for m in material(r, t)]
            shear_2 = shear + shear
            dy_vx, dz_vx = yz(o1, 0, t, r)
            dy_vy, dz_vy = yz(o1, 1, t, r)
            dy_vz, dz_vz = yz(o1, 2, t, r)
            dy_syz, dz_syz = yz(o1, 3, t, r)
            dy_syy, dz_szz = yz(o2, 0, t, r)
            dy_sxy, dz_sxz = yz(o2, 1, t, r)
            dx_vx, dx_vy, dx_vz, dx_sxx, dx_sxy, dx_sxz = (
                slopes[i, pl.ds(r, SUB), span(t)] for i in range(6)
            )
            diverge = lame * (dx_vx + dy_vy + dz_vz)
            emit(0, r, t, diverge + shear_2 * dx_vx)
            emit(1, r, t, diverge + shear_2 * dy_vy)
            emit(2, r, t, diverge + shear_2 * dz_vz)
            emit(3, r, t, shear * (dy_vx + dx_vy))
            emit(4, r, t, shear * (dz_vy + dy_vz))
            emit(5, r, t, shear * (dz_vx + dx_vz))
            emit(6, r, t, light * (dx_sxx + dy_sxy + dz_sxz))
            emit(7, r, t, light * (dx_sxy + dy_syy + dz_syz))
            emit(8, r, t, light * (dx_sxz + dy_syz + dz_szz))


def apply_operator(load, split_rows, material, tabs, scratch, rows, scale, emit):
    groups = len(scratch) // OPERATOR_SCRATCH
    size = rows // groups
    parts = [scratch[g * OPERATOR_SCRATCH : (g + 1) * OPERATOR_SCRATCH] for g in range(groups)]
    for g in range(groups):
        first = g * size
        begin_operator(
            lambda f, r, count, t: load(f, first + r, count, t),
            lambda f, t: split_rows(f, first, size, t),
            tabs,
            parts[g],
            size,
        )
    for g in range(groups):
        first = g * size
        end_operator(
            lambda r, t: material(first + r, t),
            parts[g],
            size,
            lambda r: scale(first + r),
            lambda f, r, t, value: emit(f, first + r, t, value),
        )


def span(tile):
    return slice(tile * LANES, (tile + 1) * LANES)


def pack_faces(read, rows):
    low = lane_ids(rows // 2) < HALF
    first, second = read(0, 0), read(rows // 2, 0)
    start = jnp.where(low, first, roll(second, HALF))
    first, second = read(0, 3), read(rows // 2, 3)
    end = jnp.where(low, roll(first, HALF), second)
    return end, start


def wave_speed(density, lame, shear):
    return jnp.sqrt((lame + 2.0 * shear) / density)


def early_kernel(*refs):
    sources, targets = refs[:LOADED], refs[LOADED : 2 * LOADED]
    out_ref, end_ref, start_ref = refs[2 * LOADED : 2 * LOADED + 3]
    sems, scratch = refs[2 * LOADED + 3], refs[2 * LOADED + 4 :]
    sol_ref, mat_ref, w1_ref, w2_ref, xc_ref = targets[:5]
    rows = out_ref.shape[1]
    upper, lower = pl.ds(rows, rows), pl.ds(0, rows)
    pairs = [(sources[i].at[:, upper, :], targets[i].at[:, upper, :]) for i in range(2)]
    pairs += [(sources[i], targets[i]) for i in range(2, 5)]
    pairs += [(sources[i].at[:, lower, :], targets[i].at[:, lower, :]) for i in range(2)]
    pairs += [(sources[i], targets[i]) for i in range(5, LOADED)]
    copies = [pltpu.make_async_copy(source, target, sems.at[i]) for i, (source, target) in enumerate(pairs)]
    for copy in copies:
        copy.start()
    for copy in copies[:5]:
        copy.wait()
    load = lambda f, r, count, t: sol_ref[f, rows + r : rows + r + count, span(t)]
    material = lambda r, t: (
        mat_ref[1, rows + r : rows + r + SUB, span(t)],
        mat_ref[2, rows + r : rows + r + SUB, span(t)],
        1.0 / mat_ref[0, rows + r : rows + r + SUB, span(t)],
    )

    def emit(f, r, t, value):
        base = time_step * load(f, r, SUB, t)
        out_ref[f, r : r + SUB, span(t)] = base + value

    split_rows = lambda f, r, count, t: split(load(f, r, count, t))
    tabs = (w1_ref, w2_ref, xc_ref)
    apply_operator(load, split_rows, material, tabs, scratch, rows, lambda r: taylor_weight(1), emit)
    for copy in copies[5:]:
        copy.wait()
    count = rows // 2
    for f in range(9):
        end, start = pack_faces(lambda r, t, f=f: out_ref[f, r : r + count, span(t)], rows)
        end_ref[f] = end
        start_ref[f] = start
    for i in range(2):

        def speed(r, t, i=i):
            return wave_speed(*[mat_ref[m, i * rows + r : i * rows + r + count, span(t)] for m in range(3)])

        end, start = pack_faces(speed, rows)
        end_ref[9 + i] = end
        start_ref[9 + i] = start


def refined_kernel(count_ref, sol_ref, mat_ref, w1_ref, w2_ref, xc_ref, out_ref, end_ref, start_ref, state, light, *scratch):
    rows = out_ref.shape[1]
    limit = count_ref[0, 0]
    for f in range(9):
        first = time_step * sol_ref[f, :rows, :]
        state[f] = first
        out_ref[f] = first
    light[...] = 1.0 / mat_ref[0, :rows, :]
    load = lambda f, r, count, t: state[f, r : r + count, span(t)]
    material = lambda r, t: (
        mat_ref[1, r : r + SUB, span(t)],
        mat_ref[2, r : r + SUB, span(t)],
        light[r : r + SUB, span(t)],
    )

    def emit(f, r, t, value):
        state[f, r : r + SUB, span(t)] = value
        out_ref[f, r : r + SUB, span(t)] = out_ref[f, r : r + SUB, span(t)] + value

    def term(degree, carry):
        ratio = time_step / jnp.full((SUB, LANES), degree + 1, jnp.int32).astype(jnp.float32)
        bound = jnp.where(degree < 2, rows, limit)

        def scale(r):
            ids = r + lax.broadcasted_iota(jnp.int32, (SUB, LANES), 0)
            return jnp.where(ids < bound, ratio, 0.0)

        split_rows = lambda f, r, count, t: split(state[f, r : r + count, span(t)])
        tabs = (w1_ref, w2_ref, xc_ref)
        apply_operator(load, split_rows, material, tabs, scratch, rows, scale, emit)
        return carry

    lax.fori_loop(1, ORD, term, 0)
    count = rows // 2
    for f in range(9):
        end, start = pack_faces(lambda r, t, f=f: out_ref[f, r : r + count, span(t)], rows)
        end_ref[f] = end
        start_ref[f] = start


def hot(row, first, count):
    cells = row.shape[1]
    ids = first + lax.broadcasted_iota(jnp.int32, (count, cells), 0)
    return jnp.where(ids == row, 1.0, 0.0).T


def hot_back(row):
    cells = row.shape[1]
    ids = lax.broadcasted_iota(jnp.int32, (cells, cells), 0)
    return jnp.where(ids == row, 1.0, 0.0).astype(jnp.bfloat16)


def unpack_faces(after, before):
    low = lane_ids(after.shape[0]) < HALF
    return jnp.concatenate(
        [
            jnp.where(low, after, 0.0),
            jnp.where(low, roll(after, HALF), 0.0),
            jnp.where(low, 0.0, roll(before, HALF)),
            jnp.where(low, 0.0, before),
        ],
        0,
    )


def flux(direction, jump, lame, shear, light, speed):
    members = ((6, 7, 8, 0, 3, 5), (6, 7, 8, 3, 1, 4), (6, 7, 8, 5, 4, 2))[direction]
    g = [jump[m] for m in members]
    through = g[direction]
    spread_out = lame * through
    normal = [spread_out, spread_out, spread_out, None, None, None, light * g[3], light * g[4], light * g[5]]
    normal[direction] = spread_out + 2.0 * (shear * through)
    if direction == 0:
        normal[3], normal[5] = shear * g[1], shear * g[2]
    elif direction == 1:
        normal[3], normal[4] = shear * g[0], shear * g[2]
    else:
        normal[4], normal[5] = shear * g[1], shear * g[0]
    return [
        speed * jump[f] if normal[f] is None else normal[f] + speed * jump[f] for f in range(9)
    ]


def correct_kernel(
    sol_ref, mat_ref, low_ref, high_ref, near_ref, after_ref, before_ref,
    w1_ref, w2_ref, xc_ref, squeeze_ref, spread_ref,
    out_ref, ends_ref, xmat_ref, late_ref,
    pieces, compact, xfix, hot_ref, rhs, far, fix, fixed, light, fixes, middle, sems, *scratch,
):
    cells = sol_ref.shape[1]
    half = low_ref.shape[1]
    nodes = sol_ref.shape[2]
    in_low = lane_ids(SUB) < HALF
    all_low = lane_ids(cells) < HALF
    side = jnp.where(in_low, 0.25, -0.25)

    def integral(f, r, count, t):
        if r < half:
            return low_ref[f, r : r + count, span(t)]
        return high_ref[f, r - half : r - half + count, span(t)]

    for f in range(12):
        for start in (0, half):
            at = pl.ds(f * cells + start, half)
            for t in range(TILES):
                value = integral(f, start, half, t) if f < 9 else mat_ref[f - 9, start : start + half, span(t)]
                high, low = split(value)
                pieces[at, span(t)] = high
                pieces[at, nodes + t * LANES : nodes + (t + 1) * LANES] = low
    for f in range(0, 12, 3):
        at = pl.ds(f * cells, 3 * cells)
        compact[at, :] = jnp.dot(pieces[at, :], squeeze_ref[...], preferred_element_type=jnp.float32)
    light[...] = 1.0 / mat_ref[0]

    here = near_ref[...] % cells
    for k in range(2):
        direction = k + 1
        plus = hot_back(here[2 * direction : 2 * direction + 1])
        minus = hot_back(here[2 * direction + 1 : 2 * direction + 2])
        for i in range(2):
            hot_ref[k, :, 2 * i * LANES : (2 * i + 1) * LANES] = plus
            hot_ref[k, :, (2 * i + 1) * LANES : (2 * i + 2) * LANES] = minus

        def face(f, k=k):
            return compact[pl.ds(f * cells, cells), span(k)]

        for f in range(10):
            own = face(f) if f < 9 else wave_speed(face(9), face(10), face(11))
            if f == 9:
                far[k, :, span(10)] = own
            turned = roll(own, HALF)
            for i, piece in enumerate((jnp.where(all_low, turned, 0.0), jnp.where(all_low, 0.0, turned))):
                high, low = split(piece)
                rhs[k, i * LANES : (i + 1) * LANES, span(f)] = high
                rhs[k, (i + 2) * LANES : (i + 3) * LANES, span(f)] = low
        far[k, :, : 10 * LANES] = jnp.dot(hot_ref[k], rhs[k], preferred_element_type=jnp.float32)
        for r in range(0, cells, SUB):
            at = pl.ds(r, SUB)

            def own(f, k=k, r=r):
                return compact[pl.ds(f * cells + r, SUB), span(k)]

            jump = [far[k, at, span(f)] - own(f) for f in range(9)]
            speed = 0.25 * jnp.maximum(far[k, at, span(9)], far[k, at, span(10)])
            values = flux(direction, jump, side * own(10), side * own(11), side / own(9), speed)
            for f, value in enumerate(values):
                fix[pl.ds(f * cells + r, SUB), span(k)] = value
    for f in range(9):
        at = pl.ds(f * cells, cells)
        for k in range(2):
            high, low = split(fix[at, span(k)])
            fixed[at, span(k)] = high
            fixed[at, span(k + 2)] = low

    plus, minus = here[1:2], here[0:1]
    plus, minus = hot(plus, 0, cells), hot(minus, 0, cells)
    early = jnp.concatenate([plus[:, half:], minus[:, half:]], 1).astype(jnp.bfloat16)
    late = jnp.concatenate([plus[:, :half], minus[:, :half]], 1).astype(jnp.bfloat16)
    late_ref[:, :LANES] = late
    late_ref[:, LANES:] = late
    hot_ref[2, :, 0 * LANES : 1 * LANES] = early
    hot_ref[2, :, 1 * LANES : 2 * LANES] = early
    hot_ref[2, :, 2 * LANES : 3 * LANES] = late
    hot_ref[2, :, 3 * LANES : 4 * LANES] = late
    for f in range(9):
        high, low = split(unpack_faces(after_ref[f], before_ref[f]))
        rhs[2, 0:LANES, span(f)] = high
        rhs[2, LANES : 2 * LANES, span(f)] = low
    for k, f in ((0, 10), (2, 9)):
        high, low = split(unpack_faces(after_ref[f], before_ref[f]))
        rhs[2, k * LANES : (k + 1) * LANES, span(9)] = high
        rhs[2, (k + 1) * LANES : (k + 2) * LANES, span(9)] = low
    far[2, :, : 9 * LANES] = jnp.dot(
        hot_ref[2, :, : 2 * LANES], rhs[2, : 2 * LANES, : 9 * LANES], preferred_element_type=jnp.float32
    )
    far[2, :, span(9)] = jnp.dot(hot_ref[2], rhs[2, :, span(9)], preferred_element_type=jnp.float32)
    for r in range(0, cells, SUB):
        at = pl.ds(r, SUB)
        jump = [
            far[2, at, span(f)] - jnp.where(in_low, integral(f, r, SUB, 0), integral(f, r, SUB, 3)) for f in range(9)
        ]
        density, lame, shear = (
            jnp.where(in_low, mat_ref[m, at, span(0)], mat_ref[m, at, span(3)]) for m in range(3)
        )
        speed = 0.25 * jnp.maximum(far[2, at, span(9)], wave_speed(density, lame, shear))
        lame, shear, weight = side * lame, side * shear, side / density
        for f, value in enumerate(flux(0, jump, lame, shear, weight, speed)):
            xfix[f, at, :] = value
        for i, value in enumerate((lame, shear, weight, speed)):
            xmat_ref[i, at, :] = value

    for f in range(0, 9, 3):
        at = pl.ds(f * cells, 3 * cells)
        fixes[at, :] = jnp.dot(fixed[at, :], spread_ref[...], preferred_element_type=jnp.float32)

    def split_rows(f, r, count, t):
        at = pl.ds(f * cells + r, count)
        return pieces[at, span(t)], pieces[at, nodes + t * LANES : nodes + (t + 1) * LANES]

    def material(r, t):
        at = pl.ds(r, SUB)
        return mat_ref[1, at, span(t)], mat_ref[2, at, span(t)], light[at, span(t)]

    def emit(f, r, t, value):
        at = pl.ds(r, SUB)
        total = sol_ref[f, at, span(t)] + value + fixes[pl.ds(f * cells + r, SUB), span(t)]
        if t == 0:
            ends_ref[0, f, at, :] = total + jnp.where(in_low, xfix[f, at, :], 0.0)
        elif t == TILES - 1:
            ends_ref[1, f, at, :] = total + jnp.where(in_low, 0.0, xfix[f, at, :])
        else:
            middle[f, at, span(t - 1)] = total
        if f == 8 and t == TILES - 1 and (r + SUB) % half == 0:
            stores[r // half].start()

    between = pl.ds(LANES, (TILES - 2) * LANES)
    stores = [
        pltpu.make_async_copy(
            middle.at[:, pl.ds(start, half), :], out_ref.at[:, pl.ds(start, half), between], sems.at[i]
        )
        for i, start in enumerate(range(0, cells, half))
    ]
    tabs = (w1_ref, w2_ref, xc_ref)
    apply_operator(integral, split_rows, material, tabs, scratch, cells, lambda r: None, emit)
    for copy in stores:
        copy.wait()


def finish_kernel(done_ref, ends_ref, after_ref, before_ref, xmat_ref, late_ref, out_ref, ends, rhs, far, sems):
    del done_ref
    cells = ends.shape[2]
    for f in range(9):
        high, low = split(unpack_faces(after_ref[f], before_ref[f]))
        rhs[0:LANES, span(f)] = high
        rhs[LANES : 2 * LANES, span(f)] = low
    for f in range(0, 9, 3):
        columns = slice(f * LANES, (f + 3) * LANES)
        far[:, columns] = jnp.dot(late_ref[...], rhs[:, columns], preferred_element_type=jnp.float32)
    in_low = lane_ids(SUB) < HALF
    size = cells // sems.shape[1]
    stores = []
    for r in range(0, cells, SUB):
        at = pl.ds(r, SUB)
        jump = [far[at, span(f)] for f in range(9)]
        lame, shear, weight, speed = (xmat_ref[i, at, :] for i in range(4))
        for f, value in enumerate(flux(0, jump, lame, shear, weight, speed)):
            ends[0, f, at, :] = ends_ref[0, f, at, :] + jnp.where(in_low, value, 0.0)
            ends[1, f, at, :] = ends_ref[1, f, at, :] + jnp.where(in_low, 0.0, value)
        if (r + SUB) % size == 0:
            part = pl.ds(r + SUB - size, size)
            for i, t in enumerate((0, TILES - 1)):
                copy = pltpu.make_async_copy(
                    ends.at[i, :, part, :], out_ref.at[:, part, pl.ds(t * LANES, LANES)], sems.at[i, r // size]
                )
                copy.start()
                stores.append(copy)
    for copy in stores:
        copy.wait()


def shifted(value, axis, by):
    peers = lax.axis_size(axis)
    return lax.ppermute(value, axis, [(i, (i + by) % peers) for i in range(peers)])


def f32(*shape):
    return jax.ShapeDtypeStruct(shape, jnp.float32)


def operator_scratch(rows):
    return [
        pltpu.VMEM((len(both_yz) * TILES * rows, 3 * LANES), jnp.bfloat16),
        pltpu.VMEM((len(pairs_yz) * TILES * rows, 6 * LANES), jnp.bfloat16),
        pltpu.VMEM((len(both_yz) * TILES * rows, 2 * LANES), jnp.float32),
        pltpu.VMEM((len(pairs_yz) * TILES * rows, 2 * LANES), jnp.float32),
        pltpu.VMEM((len(along_x), rows, TILES * LANES), jnp.float32),
        pltpu.VMEM((len(along_x), rows, TILES * LANES), jnp.float32),
    ]


def on_device(solution, material, neighbours, refine_count):
    cells, nodes = solution.shape[1:]
    rows = REF_MAX
    params = lambda mib: pltpu.CompilerParams(vmem_limit_bytes=mib * 1024 * 1024)
    early_shape, late_shape = (11, rows // 2, LANES), (9, rows // 2, LANES)
    in_vmem = pl.BlockSpec(memory_space=pltpu.VMEM)
    in_hbm = pl.BlockSpec(memory_space=pltpu.HBM)
    in_smem = pl.BlockSpec(memory_space=pltpu.SMEM)
    operator = operator_scratch(rows // 2) * 2

    sources = (solution, material) + tables() + face_tables()
    *loaded, high, end, start = pl.pallas_call(
        early_kernel,
        in_specs=[in_hbm] * LOADED,
        out_specs=[in_vmem] * (LOADED + 3),
        out_shape=[pltpu.VMEM(x.shape, x.dtype) for x in sources]
        + [pltpu.VMEM((9, rows, nodes), jnp.float32), f32(*early_shape), f32(*early_shape)],
        scratch_shapes=[pltpu.SemaphoreType.DMA((LOADED + 2,))] + operator,
        compiler_params=params(20),
        name="early",
    )(*[pltpu.with_memory_space_constraint(x, pltpu.HBM) for x in sources])
    sol, mat, w1, w2, xc, squeeze, spread = loaded
    early_after = shifted(end, "space", -1)
    early_before = shifted(start, "space", 1)

    low, end, start = pl.pallas_call(
        refined_kernel,
        in_specs=[in_smem] + [in_vmem] * 5,
        out_specs=[in_vmem] * 3,
        out_shape=[pltpu.VMEM((9, rows, nodes), jnp.float32), f32(*late_shape), f32(*late_shape)],
        scratch_shapes=[
            pltpu.VMEM((9, rows, nodes), jnp.float32),
            pltpu.VMEM((rows, nodes), jnp.float32),
        ]
        + operator,
        compiler_params=params(20),
        name="refined",
    )(refine_count, sol, mat, w1, w2, xc)
    late_after = shifted(end, "space", -1)
    late_before = shifted(start, "space", 1)

    done, ends, xmat, late_hot = pl.pallas_call(
        correct_kernel,
        in_specs=[in_vmem] * 12,
        out_specs=[in_hbm] + [in_vmem] * 3,
        out_shape=[
            pltpu.HBM(solution.shape, jnp.float32),
            pltpu.VMEM((2, 9, cells, LANES), jnp.float32),
            pltpu.VMEM((4, cells, LANES), jnp.float32),
            pltpu.VMEM((cells, 2 * LANES), jnp.bfloat16),
        ],
        scratch_shapes=[
            pltpu.VMEM((12 * cells, 2 * nodes), jnp.bfloat16),
            pltpu.VMEM((12 * cells, 2 * LANES), jnp.float32),
            pltpu.VMEM((9, cells, LANES), jnp.float32),
            pltpu.VMEM((3, cells, 4 * LANES), jnp.bfloat16),
            pltpu.VMEM((3, 4 * LANES, 10 * LANES), jnp.bfloat16),
            pltpu.VMEM((3, cells, 11 * LANES), jnp.float32),
            pltpu.VMEM((9 * cells, 2 * LANES), jnp.float32),
            pltpu.VMEM((9 * cells, 4 * LANES), jnp.bfloat16),
            pltpu.VMEM((cells, nodes), jnp.float32),
            pltpu.VMEM((9 * cells, nodes), jnp.float32),
            pltpu.VMEM((9, cells, nodes - 2 * LANES), jnp.float32),
            pltpu.SemaphoreType.DMA((2,)),
        ]
        + operator_scratch(rows) * 2,
        compiler_params=params(40),
        name="correct",
    )(sol, mat, low, high, neighbours, early_after, early_before, w1, w2, xc, squeeze, spread)

    return pl.pallas_call(
        finish_kernel,
        in_specs=[in_hbm] + [in_vmem] * 5,
        out_specs=in_hbm,
        out_shape=f32(*solution.shape),
        scratch_shapes=[
            pltpu.VMEM((2, 9, cells, LANES), jnp.float32),
            pltpu.VMEM((2 * LANES, 9 * LANES), jnp.bfloat16),
            pltpu.VMEM((cells, 9 * LANES), jnp.float32),
            pltpu.SemaphoreType.DMA((2, 4)),
        ],
        input_output_aliases={0: 0},
        compiler_params=params(8),
        name="finish",
    )(done, ends, late_after, late_before, xmat, late_hot)


def solution(mesh):
    in_specs = (
        P(None, ("space", "help"), None),
        P(None, ("space", "help"), None),
        P(None, ("space", "help")),
        P("space", "help"),
    )
    out_specs = P(None, ("space", "help"), None)
    return jax.shard_map(
        on_device, mesh=mesh, in_specs=in_specs, out_specs=out_specs, check_vma=False
    )
```

```python
import math

import jax
import jax.numpy as jnp
import ml_dtypes
import numpy as np
from jax import lax
from jax.experimental import pallas as pl
from jax.experimental.pallas import tpu as pltpu
from jax.sharding import PartitionSpec as P

P_SIZE = 8
ORD = 8
REF_MAX = 64
LANES = 128
TILES = 4
HALF = 64
SUB = 8
PACK = 16
LOADED = 7

along_x = (6, 7, 8, 0, 3, 5)
along_y = (6, 7, 8, 3, 1, 4)
along_z = (6, 7, 8, 5, 4, 2)
both_yz = (6, 7, 8, 4)
pairs_yz = ((1, 2), (3, 5))
time_step = 0.5


def cheb_table(node_count):
    intervals = node_count - 1
    places = np.arange(node_count)
    points = np.cos(np.pi * places / intervals)
    weights = np.where((places == 0) | (places == intervals), 2.0, 1.0)
    scaled = weights * (-1.0) ** places
    differ = points[:, None] - points[None, :] + np.eye(node_count)
    matrix = np.outer(scaled, 1.0 / scaled) / differ
    matrix = matrix - np.eye(node_count) * np.sum(matrix, axis=1)[:, None]
    return matrix / (node_count * node_count / 4.0)


def taylor_weight(degree):
    return time_step ** (degree + 1) / math.factorial(degree + 1)


def tables():
    slope = cheb_table(P_SIZE).astype(np.float32).astype(np.float64)
    high = slope.astype(ml_dtypes.bfloat16).astype(np.float64)
    low = slope - high
    one = np.eye(P_SIZE)
    two = np.eye(2)

    def spread(matrix):
        along_b = np.kron(two, np.kron(matrix.T, one))
        along_e = np.kron(two, np.kron(one, matrix.T))
        return along_b, along_e

    hy, hz = spread(high)
    ly, lz = spread(low)
    none = np.zeros_like(hy)
    w1 = np.concatenate(
        [np.concatenate([hy, hz], 1), np.concatenate([hy, hz], 1), np.concatenate([ly, lz], 1)], 0
    )
    diag_high = np.block([[hy, none], [none, hz]])
    diag_low = np.block([[ly, none], [none, lz]])
    w2 = np.concatenate([diag_high, diag_high, diag_low], 0)

    half = P_SIZE // 2
    top = slope[:half, :half]
    mirror = slope[:half, ::-1][:, :half]
    lane_half = np.arange(LANES) // HALF
    rows = []
    for part in ((top + mirror) / 2, (top - mirror) / 2):
        for t in range(2):
            for s in range(2):
                for source in (lane_half, 1 - lane_half):
                    rows.append(part[2 * t + lane_half, 2 * s + source])
    xc = np.broadcast_to(np.stack(rows)[:, None, :], (len(rows), SUB, LANES))
    return (
        jnp.asarray(w1.astype(ml_dtypes.bfloat16)),
        jnp.asarray(w2.astype(ml_dtypes.bfloat16)),
        jnp.asarray(np.ascontiguousarray(xc).astype(np.float32)),
    )


def face_tables():
    node = np.arange(P_SIZE**3)
    places = (node // P_SIZE % P_SIZE, node % P_SIZE)
    others = (
        node // HALF * P_SIZE + node % P_SIZE,
        (node // HALF + P_SIZE // 2) % P_SIZE * P_SIZE + node // P_SIZE % P_SIZE,
    )
    pick = np.zeros((P_SIZE**3, 2 * LANES))
    for k in range(2):
        for side, place in enumerate((0, P_SIZE - 1)):
            on = places[k] == place
            pick[node[on], k * LANES + side * HALF + others[k][on]] = 1.0
    squeeze = np.concatenate([pick, pick], 0).astype(ml_dtypes.bfloat16)
    in_first = np.arange(LANES) % HALF < HALF // 2
    both = []
    for part in range(2):
        keep_y = in_first if part == 0 else ~in_first
        mixed = np.where(keep_y[None, :], pick[:, :LANES], pick[:, LANES:])
        piece = mixed[part * 2 * LANES : (part + 1) * 2 * LANES].T
        both += [piece, piece]
    spread = np.concatenate(both, 0).astype(ml_dtypes.bfloat16)
    return jnp.asarray(squeeze), jnp.asarray(spread)


def roll(value, by):
    by = by % LANES
    return value if by == 0 else pltpu.roll(value, by, value.ndim - 1)


def lane_ids(rows):
    return lax.broadcasted_iota(jnp.int32, (rows, LANES), 1)


def split(value):
    high = value.astype(jnp.bfloat16)
    return high, (value - high.astype(jnp.float32)).astype(jnp.bfloat16)


def turn(load, r):
    return [[roll(load(f, r, SUB, t), HALF) for t in range(TILES)] for f in along_x]


def x_slope(own, other, xc_ref):
    sums = [[], []]
    for kind in range(2):
        sources = []
        for s in range(2):
            if kind == 0:
                sources.append((own[s] + other[3 - s], other[s] + own[3 - s]))
            else:
                sources.append((own[s] - other[3 - s], other[s] - own[3 - s]))
        for t in range(2):
            total = None
            for s in range(2):
                for swap in range(2):
                    term = sources[s][swap] * xc_ref[((kind * 2 + t) * 2 + s) * 2 + swap]
                    total = term if total is None else total + term
            sums[kind].append(total)
    slopes = [None] * TILES
    for t in range(2):
        even, odd = sums[0][t], sums[1][t]
        slopes[t] = even + odd
        slopes[3 - t] = roll(odd - even, HALF)
    return slopes


def begin_operator(split_rows, tabs, first, rows):
    w1_ref, w2_ref, _ = tabs
    left, right = [], []
    for r in range(first, first + rows, PACK):
        for t in range(TILES):
            parts = {f: split_rows(f, r, PACK, t) for f in both_yz + pairs_yz[0] + pairs_yz[1]}
            for f in both_yz:
                high, low = parts[f]
                left.append(jnp.concatenate([high, low, high], 1))
            for f, g in pairs_yz:
                (high_f, low_f), (high_g, low_g) = parts[f], parts[g]
                right.append(jnp.concatenate([high_f, high_g, low_f, low_g, high_f, high_g], 1))
    left, right = jnp.concatenate(left, 0), jnp.concatenate(right, 0)
    return (
        jnp.dot(left, w1_ref[...], preferred_element_type=jnp.float32),
        jnp.dot(right, w2_ref[...], preferred_element_type=jnp.float32),
    )


def end_operator(load, material, tabs, products, first, rows, scale, emit):
    xc_ref = tabs[2]
    o1, o2 = products

    def yz(values, count, i, t, r):
        at = (((r - first) // PACK * TILES + t) * count + i) * PACK + r % PACK
        return values[at : at + SUB, :LANES], values[at : at + SUB, LANES:]

    following = turn(load, first)
    for r in range(first, first + rows, SUB):
        turned = following
        if r + SUB < first + rows:
            following = turn(load, r + SUB)
        slopes = [
            x_slope([load(f, r, SUB, t) for t in range(TILES)], turned[i], xc_ref) for i, f in enumerate(along_x)
        ]
        factor = scale(r)
        for t in range(TILES):
            lame, shear, light = [m if factor is None else m * factor for m in material(r, t)]
            shear_2 = shear + shear
            dy_vx, dz_vx = yz(o1, 4, 0, t, r)
            dy_vy, dz_vy = yz(o1, 4, 1, t, r)
            dy_vz, dz_vz = yz(o1, 4, 2, t, r)
            dy_syz, dz_syz = yz(o1, 4, 3, t, r)
            dy_syy, dz_szz = yz(o2, 2, 0, t, r)
            dy_sxy, dz_sxz = yz(o2, 2, 1, t, r)
            dx_vx, dx_vy, dx_vz, dx_sxx, dx_sxy, dx_sxz = (slope[t] for slope in slopes)
            diverge = lame * (dx_vx + dy_vy + dz_vz)
            emit(0, r, t, diverge + shear_2 * dx_vx)
            emit(1, r, t, diverge + shear_2 * dy_vy)
            emit(2, r, t, diverge + shear_2 * dz_vz)
            emit(3, r, t, shear * (dy_vx + dx_vy))
            emit(4, r, t, shear * (dz_vy + dy_vz))
            emit(5, r, t, shear * (dz_vx + dx_vz))
            emit(6, r, t, light * (dx_sxx + dy_sxy + dz_sxz))
            emit(7, r, t, light * (dx_sxy + dy_syy + dz_syz))
            emit(8, r, t, light * (dx_sxz + dy_syz + dz_szz))


def apply_operator(load, split_rows, material, tabs, rows, size, scale, emit):
    groups = range(0, rows, size)
    products = [begin_operator(split_rows, tabs, first, size) for first in groups]
    for first, product in zip(groups, products):
        end_operator(load, material, tabs, product, first, size, scale, emit)


def span(tile):
    return slice(tile * LANES, (tile + 1) * LANES)


def pack_faces(read, rows):
    low = lane_ids(rows // 2) < HALF
    first, second = read(0, 0), read(rows // 2, 0)
    start = jnp.where(low, first, roll(second, HALF))
    first, second = read(0, 3), read(rows // 2, 3)
    end = jnp.where(low, roll(first, HALF), second)
    return end, start


def odd_device():
    return lax.rem(lax.axis_index("space"), 2) == 1


def send_faces(odd, near_ref, far_ref, index, end, start):
    near_ref[index] = jnp.where(odd, end, start)
    far_ref[index] = jnp.where(odd, start, end)


def got_faces(odd, near_ref, far_ref, index):
    near, far = near_ref[index], far_ref[index]
    return jnp.where(odd, far, near), jnp.where(odd, near, far)


def wave_speed(density, lame, shear):
    return jnp.sqrt((lame + 2.0 * shear) / density)


def early_kernel(*refs):
    sources, targets = refs[:LOADED], refs[LOADED : 2 * LOADED]
    out_ref, near_ref, far_ref = refs[2 * LOADED : 2 * LOADED + 3]
    sems = refs[2 * LOADED + 3]
    sol_ref, mat_ref, w1_ref, w2_ref, xc_ref = targets[:5]
    rows = out_ref.shape[1]
    upper, lower = pl.ds(rows, rows), pl.ds(0, rows)
    pairs = [(sources[i].at[:, upper, :], targets[i].at[:, upper, :]) for i in range(2)]
    pairs += [(sources[i], targets[i]) for i in range(2, 5)]
    pairs += [(sources[i].at[:, lower, :], targets[i].at[:, lower, :]) for i in range(2)]
    pairs += [(sources[i], targets[i]) for i in range(5, LOADED)]
    copies = [pltpu.make_async_copy(source, target, sems.at[i]) for i, (source, target) in enumerate(pairs)]
    for copy in copies:
        copy.start()
    for copy in copies[:5]:
        copy.wait()
    load = lambda f, r, count, t: sol_ref[f, rows + r : rows + r + count, span(t)]
    material = lambda r, t: (
        mat_ref[1, rows + r : rows + r + SUB, span(t)],
        mat_ref[2, rows + r : rows + r + SUB, span(t)],
        1.0 / mat_ref[0, rows + r : rows + r + SUB, span(t)],
    )

    def emit(f, r, t, value):
        base = time_step * load(f, r, SUB, t)
        out_ref[f, r : r + SUB, span(t)] = base + value

    split_rows = lambda f, r, count, t: split(load(f, r, count, t))
    tabs = (w1_ref, w2_ref, xc_ref)
    apply_operator(load, split_rows, material, tabs, rows, rows // 2, lambda r: taylor_weight(1), emit)
    for copy in copies[5:]:
        copy.wait()
    count = rows // 2
    odd = odd_device()
    for f in range(9):
        end, start = pack_faces(lambda r, t, f=f: out_ref[f, r : r + count, span(t)], rows)
        send_faces(odd, near_ref, far_ref, f, end, start)
    for i in range(2):

        def speed(r, t, i=i):
            return wave_speed(*[mat_ref[m, i * rows + r : i * rows + r + count, span(t)] for m in range(3)])

        end, start = pack_faces(speed, rows)
        send_faces(odd, near_ref, far_ref, 9 + i, end, start)


def refined_kernel(count_ref, sol_ref, mat_ref, w1_ref, w2_ref, xc_ref, out_ref, near_ref, far_ref, state, light):
    rows = out_ref.shape[1]
    limit = jnp.broadcast_to(count_ref[...], (SUB, LANES))
    light[...] = 1.0 / mat_ref[0, :rows, :]
    tabs = (w1_ref, w2_ref, xc_ref)
    material = lambda r, t: (
        mat_ref[1, r : r + SUB, span(t)],
        mat_ref[2, r : r + SUB, span(t)],
        light[r : r + SUB, span(t)],
    )

    def next_term(source, scale, first):
        load = lambda f, r, count, t: source[f, r : r + count, span(t)]
        split_rows = lambda f, r, count, t: split(load(f, r, count, t))

        def emit(f, r, t, value):
            at = pl.ds(r, SUB)
            before = time_step * sol_ref[f, at, span(t)] if first else out_ref[f, at, span(t)]
            state[f, at, span(t)] = value
            out_ref[f, at, span(t)] = before + value

        apply_operator(load, split_rows, material, tabs, rows, rows // 2, scale, emit)

    def term(degree, carry):
        ratio = time_step / jnp.full((SUB, LANES), degree + 1, jnp.int32).astype(jnp.float32)

        def scale(r):
            ids = r + lax.broadcasted_iota(jnp.int32, (SUB, LANES), 0)
            return jnp.where(ids < limit, ratio, 0.0)

        next_term(state, scale, False)
        return carry

    next_term(sol_ref, lambda r: taylor_weight(1), True)
    lax.fori_loop(2, ORD, term, 0)
    count = rows // 2
    odd = odd_device()
    for f in range(9):
        end, start = pack_faces(lambda r, t, f=f: out_ref[f, r : r + count, span(t)], rows)
        send_faces(odd, near_ref, far_ref, f, end, start)


def hot(row, first, count):
    cells = row.shape[1]
    ids = first + lax.broadcasted_iota(jnp.int32, (count, cells), 0)
    return jnp.where(ids == row, 1.0, 0.0).T


def hot_back(row):
    cells = row.shape[1]
    ids = lax.broadcasted_iota(jnp.int32, (cells, cells), 0)
    return jnp.where(ids == row, 1.0, 0.0).astype(jnp.bfloat16)


def unpack_faces(after, before):
    low = lane_ids(after.shape[0]) < HALF
    return jnp.concatenate(
        [
            jnp.where(low, after, 0.0),
            jnp.where(low, roll(after, HALF), 0.0),
            jnp.where(low, 0.0, roll(before, HALF)),
            jnp.where(low, 0.0, before),
        ],
        0,
    )


def flux(direction, jump, lame, shear, light, speed):
    members = ((6, 7, 8, 0, 3, 5), (6, 7, 8, 3, 1, 4), (6, 7, 8, 5, 4, 2))[direction]
    g = [jump[m] for m in members]
    through = g[direction]
    spread_out = lame * through
    normal = [spread_out, spread_out, spread_out, None, None, None, light * g[3], light * g[4], light * g[5]]
    normal[direction] = spread_out + 2.0 * (shear * through)
    if direction == 0:
        normal[3], normal[5] = shear * g[1], shear * g[2]
    elif direction == 1:
        normal[3], normal[4] = shear * g[0], shear * g[2]
    else:
        normal[4], normal[5] = shear * g[1], shear * g[0]
    return [
        speed * jump[f] if normal[f] is None else normal[f] + speed * jump[f] for f in range(9)
    ]


def correct_kernel(
    sol_ref, mat_ref, low_ref, high_ref, beside_ref, near_ref, far_ref,
    w1_ref, w2_ref, xc_ref, squeeze_ref, spread_ref,
    out_ref, ends_ref, xmat_ref, late_ref,
    pieces, compact, xfix, hot_ref, rhs, far, fix, fixed, light, fixes, middle, sems,
):
    cells = sol_ref.shape[1]
    half = low_ref.shape[1]
    nodes = sol_ref.shape[2]
    in_low = lane_ids(SUB) < HALF
    all_low = lane_ids(cells) < HALF
    in_first = lane_ids(cells) % HALF < HALF // 2
    side = jnp.where(in_low, 0.25, -0.25)

    def integral(f, r, count, t):
        if r < half:
            return low_ref[f, r : r + count, span(t)]
        return high_ref[f, r - half : r - half + count, span(t)]

    for f in range(12):
        for start in (0, half):
            at = pl.ds(f * cells + start, half)
            for t in range(TILES):
                value = integral(f, start, half, t) if f < 9 else mat_ref[f - 9, start : start + half, span(t)]
                high, low = split(value)
                pieces[at, span(t)] = high
                pieces[at, nodes + t * LANES : nodes + (t + 1) * LANES] = low
    for f in range(0, 12, 3):
        at = pl.ds(f * cells, 3 * cells)
        compact[at, :] = jnp.dot(pieces[at, :], squeeze_ref[...], preferred_element_type=jnp.float32)
    light[...] = 1.0 / mat_ref[0]

    here = beside_ref[...] % cells
    odd = odd_device()
    for k in range(2):
        direction = k + 1
        plus = hot_back(here[2 * direction : 2 * direction + 1])
        minus = hot_back(here[2 * direction + 1 : 2 * direction + 2])
        for i in range(2):
            hot_ref[k, :, 2 * i * LANES : (2 * i + 1) * LANES] = plus
            hot_ref[k, :, (2 * i + 1) * LANES : (2 * i + 2) * LANES] = minus

        def face(f, k=k):
            return compact[pl.ds(f * cells, cells), span(k)]

        for f in range(10):
            own = face(f) if f < 9 else wave_speed(face(9), face(10), face(11))
            if f == 9:
                far[k, :, span(10)] = own
            turned = roll(own, HALF)
            for i, piece in enumerate((jnp.where(all_low, turned, 0.0), jnp.where(all_low, 0.0, turned))):
                high, low = split(piece)
                rhs[k, i * LANES : (i + 1) * LANES, span(f)] = high
                rhs[k, (i + 2) * LANES : (i + 3) * LANES, span(f)] = low
        far[k, :, : 10 * LANES] = jnp.dot(hot_ref[k], rhs[k], preferred_element_type=jnp.float32)
        for r in range(0, cells, SUB):
            at = pl.ds(r, SUB)

            def own(f, k=k, r=r):
                return compact[pl.ds(f * cells + r, SUB), span(k)]

            jump = [far[k, at, span(f)] - own(f) for f in range(9)]
            speed = 0.25 * jnp.maximum(far[k, at, span(9)], far[k, at, span(10)])
            values = flux(direction, jump, side * own(10), side * own(11), side / own(9), speed)
            for f, value in enumerate(values):
                fix[pl.ds(f * cells + r, SUB), span(k)] = value
    for f in range(9):
        at = pl.ds(f * cells, cells)
        along, across = fix[at, span(0)], fix[at, span(1)]
        for k, value in enumerate((jnp.where(in_first, along, across), jnp.where(in_first, across, along))):
            high, low = split(value)
            fixed[at, span(2 * k)] = high
            fixed[at, span(2 * k + 1)] = low

    plus, minus = here[1:2], here[0:1]
    plus, minus = hot(plus, 0, cells), hot(minus, 0, cells)
    early = jnp.concatenate([plus[:, half:], minus[:, half:]], 1).astype(jnp.bfloat16)
    late = jnp.concatenate([plus[:, :half], minus[:, :half]], 1).astype(jnp.bfloat16)
    late_ref[:, :LANES] = late
    late_ref[:, LANES:] = late
    hot_ref[2, :, 0 * LANES : 1 * LANES] = early
    hot_ref[2, :, 1 * LANES : 2 * LANES] = early
    hot_ref[2, :, 2 * LANES : 3 * LANES] = late
    hot_ref[2, :, 3 * LANES : 4 * LANES] = late
    for f in range(9):
        high, low = split(unpack_faces(*got_faces(odd, near_ref, far_ref, f)))
        rhs[2, 0:LANES, span(f)] = high
        rhs[2, LANES : 2 * LANES, span(f)] = low
    for k, f in ((0, 10), (2, 9)):
        high, low = split(unpack_faces(*got_faces(odd, near_ref, far_ref, f)))
        rhs[2, k * LANES : (k + 1) * LANES, span(9)] = high
        rhs[2, (k + 1) * LANES : (k + 2) * LANES, span(9)] = low
    far[2, :, : 9 * LANES] = jnp.dot(
        hot_ref[2, :, : 2 * LANES], rhs[2, : 2 * LANES, : 9 * LANES], preferred_element_type=jnp.float32
    )
    far[2, :, span(9)] = jnp.dot(hot_ref[2], rhs[2, :, span(9)], preferred_element_type=jnp.float32)
    for r in range(0, cells, SUB):
        at = pl.ds(r, SUB)
        jump = [
            far[2, at, span(f)] - jnp.where(in_low, integral(f, r, SUB, 0), integral(f, r, SUB, 3)) for f in range(9)
        ]
        density, lame, shear = (
            jnp.where(in_low, mat_ref[m, at, span(0)], mat_ref[m, at, span(3)]) for m in range(3)
        )
        speed = 0.25 * jnp.maximum(far[2, at, span(9)], wave_speed(density, lame, shear))
        lame, shear, weight = side * lame, side * shear, side / density
        for f, value in enumerate(flux(0, jump, lame, shear, weight, speed)):
            xfix[f, at, :] = value
        for i, value in enumerate((lame, shear, weight, speed)):
            xmat_ref[i, at, :] = value

    for k in range(2):
        at = slice(2 * k * LANES, 2 * (k + 1) * LANES)
        fixes[:, at] = jnp.dot(fixed[:, at], spread_ref[at, :], preferred_element_type=jnp.float32)

    def split_rows(f, r, count, t):
        at = pl.ds(f * cells + r, count)
        return pieces[at, span(t)], pieces[at, nodes + t * LANES : nodes + (t + 1) * LANES]

    def material(r, t):
        at = pl.ds(r, SUB)
        return mat_ref[1, at, span(t)], mat_ref[2, at, span(t)], light[at, span(t)]

    def emit(f, r, t, value):
        at = pl.ds(r, SUB)
        total = sol_ref[f, at, span(t)] + value + fixes[pl.ds(f * cells + r, SUB), span(t)]
        if t == 0:
            ends_ref[0, f, at, :] = total + jnp.where(in_low, xfix[f, at, :], 0.0)
        elif t == TILES - 1:
            ends_ref[1, f, at, :] = total + jnp.where(in_low, 0.0, xfix[f, at, :])
        else:
            middle[f, at, span(t - 1)] = total
        if f == 8 and t == TILES - 1 and (r + SUB) % half == 0:
            stores[r // half].start()

    between = pl.ds(LANES, (TILES - 2) * LANES)
    stores = [
        pltpu.make_async_copy(
            middle.at[:, pl.ds(start, half), :], out_ref.at[:, pl.ds(start, half), between], sems.at[i]
        )
        for i, start in enumerate(range(0, cells, half))
    ]
    tabs = (w1_ref, w2_ref, xc_ref)
    apply_operator(integral, split_rows, material, tabs, cells, half, lambda r: None, emit)
    for copy in stores:
        copy.wait()


def finish_kernel(done_ref, ends_ref, near_ref, far_ref, xmat_ref, late_ref, out_ref, ends, rhs, far, sems):
    del done_ref
    cells = ends.shape[2]
    odd = odd_device()
    for f in range(9):
        high, low = split(unpack_faces(*got_faces(odd, near_ref, far_ref, f)))
        rhs[0:LANES, span(f)] = high
        rhs[LANES : 2 * LANES, span(f)] = low
    for f in range(0, 9, 3):
        columns = slice(f * LANES, (f + 3) * LANES)
        far[:, columns] = jnp.dot(late_ref[...], rhs[:, columns], preferred_element_type=jnp.float32)
    in_low = lane_ids(SUB) < HALF
    size = cells // sems.shape[1]
    stores = []
    for r in range(0, cells, SUB):
        at = pl.ds(r, SUB)
        jump = [far[at, span(f)] for f in range(9)]
        lame, shear, weight, speed = (xmat_ref[i, at, :] for i in range(4))
        for f, value in enumerate(flux(0, jump, lame, shear, weight, speed)):
            ends[0, f, at, :] = ends_ref[0, f, at, :] + jnp.where(in_low, value, 0.0)
            ends[1, f, at, :] = ends_ref[1, f, at, :] + jnp.where(in_low, 0.0, value)
        if (r + SUB) % size == 0:
            part = pl.ds(r + SUB - size, size)
            for i, t in enumerate((0, TILES - 1)):
                copy = pltpu.make_async_copy(
                    ends.at[i, :, part, :], out_ref.at[:, part, pl.ds(t * LANES, LANES)], sems.at[i, r // size]
                )
                copy.start()
                stores.append(copy)
    for copy in stores:
        copy.wait()


def exchange(near, far):
    peers = lax.axis_size("space")
    got_near = lax.ppermute(near, "space", [(i, i + (-1 if i % 2 else 1)) for i in range(peers)])
    got_far = lax.ppermute(far, "space", [(i, (i + (1 if i % 2 else -1)) % peers) for i in range(peers)])
    return got_near, got_far


def f32(*shape):
    return jax.ShapeDtypeStruct(shape, jnp.float32)


def on_device(solution, material, neighbours, refine_count):
    cells, nodes = solution.shape[1:]
    rows = REF_MAX
    params = lambda mib: pltpu.CompilerParams(vmem_limit_bytes=mib * 1024 * 1024)
    early_shape, late_shape = (11, rows // 2, LANES), (9, rows // 2, LANES)
    in_vmem = pl.BlockSpec(memory_space=pltpu.VMEM)
    in_hbm = pl.BlockSpec(memory_space=pltpu.HBM)

    sources = (solution, material) + tables() + face_tables()
    *loaded, high, near, far = pl.pallas_call(
        early_kernel,
        in_specs=[in_hbm] * LOADED,
        out_specs=[in_vmem] * (LOADED + 3),
        out_shape=[pltpu.VMEM(x.shape, x.dtype) for x in sources]
        + [pltpu.VMEM((9, rows, nodes), jnp.float32), f32(*early_shape), f32(*early_shape)],
        scratch_shapes=[pltpu.SemaphoreType.DMA((LOADED + 2,))],
        compiler_params=params(20),
        name="early",
    )(*[pltpu.with_memory_space_constraint(x, pltpu.HBM) for x in sources])
    sol, mat, w1, w2, xc, squeeze, spread = loaded
    early_near, early_far = exchange(near, far)

    low, near, far = pl.pallas_call(
        refined_kernel,
        in_specs=[in_vmem] * 6,
        out_specs=[in_vmem] * 3,
        out_shape=[pltpu.VMEM((9, rows, nodes), jnp.float32), f32(*late_shape), f32(*late_shape)],
        scratch_shapes=[
            pltpu.VMEM((9, rows, nodes), jnp.float32),
            pltpu.VMEM((rows, nodes), jnp.float32),
        ],
        compiler_params=params(20),
        name="refined",
    )(refine_count, sol, mat, w1, w2, xc)
    late_near, late_far = exchange(near, far)

    done, ends, xmat, late_hot = pl.pallas_call(
        correct_kernel,
        in_specs=[in_vmem] * 12,
        out_specs=[in_hbm] + [in_vmem] * 3,
        out_shape=[
            pltpu.HBM(solution.shape, jnp.float32),
            pltpu.VMEM((2, 9, cells, LANES), jnp.float32),
            pltpu.VMEM((4, cells, LANES), jnp.float32),
            pltpu.VMEM((cells, 2 * LANES), jnp.bfloat16),
        ],
        scratch_shapes=[
            pltpu.VMEM((12 * cells, 2 * nodes), jnp.bfloat16),
            pltpu.VMEM((12 * cells, 2 * LANES), jnp.float32),
            pltpu.VMEM((9, cells, LANES), jnp.float32),
            pltpu.VMEM((3, cells, 4 * LANES), jnp.bfloat16),
            pltpu.VMEM((3, 4 * LANES, 10 * LANES), jnp.bfloat16),
            pltpu.VMEM((3, cells, 11 * LANES), jnp.float32),
            pltpu.VMEM((9 * cells, 2 * LANES), jnp.float32),
            pltpu.VMEM((9 * cells, 4 * LANES), jnp.bfloat16),
            pltpu.VMEM((cells, nodes), jnp.float32),
            pltpu.VMEM((9 * cells, nodes), jnp.float32),
            pltpu.VMEM((9, cells, nodes - 2 * LANES), jnp.float32),
            pltpu.SemaphoreType.DMA((2,)),
        ],
        compiler_params=params(40),
        name="correct",
    )(sol, mat, low, high, neighbours, early_near, early_far, w1, w2, xc, squeeze, spread)

    return pl.pallas_call(
        finish_kernel,
        in_specs=[in_hbm] + [in_vmem] * 5,
        out_specs=in_hbm,
        out_shape=f32(*solution.shape),
        scratch_shapes=[
            pltpu.VMEM((2, 9, cells, LANES), jnp.float32),
            pltpu.VMEM((2 * LANES, 9 * LANES), jnp.bfloat16),
            pltpu.VMEM((cells, 9 * LANES), jnp.float32),
            pltpu.SemaphoreType.DMA((2, 4)),
        ],
        input_output_aliases={0: 0},
        compiler_params=params(8),
        name="finish",
    )(done, ends, late_near, late_far, xmat, late_hot)


def solution(mesh):
    in_specs = (
        P(None, ("space", "help"), None),
        P(None, ("space", "help"), None),
        P(None, ("space", "help")),
        P("space", "help"),
    )
    out_specs = P(None, ("space", "help"), None)
    return jax.shard_map(
        on_device, mesh=mesh, in_specs=in_specs, out_specs=out_specs, check_vma=False
    )
```

```python
import functools
import math

import jax
import jax.numpy as jnp
import ml_dtypes
import numpy as np
from jax import lax
from jax.experimental import pallas as pl
from jax.experimental.pallas import tpu as pltpu
from jax.sharding import PartitionSpec as P

P_SIZE = 8
ORD = 8
REF_MAX = 64
LANES = 128
TILES = 4
HALF = 64
SUB = 8
PACK = 16
LOADED = 5

along_x = (6, 7, 8, 0, 3, 5)
along_y = (6, 7, 8, 3, 1, 4)
along_z = (6, 7, 8, 5, 4, 2)
both_yz = (6, 7, 8, 4)
pairs_yz = ((1, 2), (3, 5))
time_step = 0.5


def cheb_table(node_count):
    intervals = node_count - 1
    places = np.arange(node_count)
    points = np.cos(np.pi * places / intervals)
    weights = np.where((places == 0) | (places == intervals), 2.0, 1.0)
    scaled = weights * (-1.0) ** places
    differ = points[:, None] - points[None, :] + np.eye(node_count)
    matrix = np.outer(scaled, 1.0 / scaled) / differ
    matrix = matrix - np.eye(node_count) * np.sum(matrix, axis=1)[:, None]
    return matrix / (node_count * node_count / 4.0)


def taylor_weight(degree):
    return time_step ** (degree + 1) / math.factorial(degree + 1)


def tables():
    slope = cheb_table(P_SIZE).astype(np.float32).astype(np.float64)
    high = slope.astype(ml_dtypes.bfloat16).astype(np.float64)
    low = slope - high
    one = np.eye(P_SIZE)
    two = np.eye(2)

    def spread(matrix):
        along_b = np.kron(two, np.kron(matrix.T, one))
        along_e = np.kron(two, np.kron(one, matrix.T))
        return along_b, along_e

    hy, hz = spread(high)
    ly, lz = spread(low)
    none = np.zeros_like(hy)
    w1 = np.concatenate(
        [np.concatenate([hy, hz], 1), np.concatenate([hy, hz], 1), np.concatenate([ly, lz], 1)], 0
    )
    diag_high = np.block([[hy, none], [none, hz]])
    diag_low = np.block([[ly, none], [none, lz]])
    w2 = np.concatenate([diag_high, diag_high, diag_low], 0)

    half = P_SIZE // 2
    top = slope[:half, :half]
    mirror = slope[:half, ::-1][:, :half]
    lane_half = np.arange(LANES) // HALF
    rows = []
    for part in ((top + mirror) / 2, (top - mirror) / 2):
        for t in range(2):
            for s in range(2):
                for source in (lane_half, 1 - lane_half):
                    rows.append(part[2 * t + lane_half, 2 * s + source])
    xc = np.broadcast_to(np.stack(rows)[:, None, :], (len(rows), SUB, LANES))
    return (
        jnp.asarray(w1.astype(ml_dtypes.bfloat16)),
        jnp.asarray(w2.astype(ml_dtypes.bfloat16)),
        jnp.asarray(np.ascontiguousarray(xc).astype(np.float32)),
    )


def face_tables():
    node = np.arange(P_SIZE**3)
    places = (node // P_SIZE % P_SIZE, node % P_SIZE)
    others = (
        node // HALF * P_SIZE + node % P_SIZE,
        (node // HALF + P_SIZE // 2) % P_SIZE * P_SIZE + node // P_SIZE % P_SIZE,
    )
    pick = np.zeros((P_SIZE**3, 2 * LANES))
    for k in range(2):
        for side, place in enumerate((0, P_SIZE - 1)):
            on = places[k] == place
            pick[node[on], k * LANES + side * HALF + others[k][on]] = 1.0
    squeeze = np.concatenate([pick, pick], 0).astype(ml_dtypes.bfloat16)
    in_first = np.arange(LANES) % HALF < HALF // 2
    both = []
    for part in range(2):
        keep_y = in_first if part == 0 else ~in_first
        mixed = np.where(keep_y[None, :], pick[:, :LANES], pick[:, LANES:])
        piece = mixed[part * 2 * LANES : (part + 1) * 2 * LANES].T
        both += [piece, piece]
    spread = np.concatenate(both, 0).astype(ml_dtypes.bfloat16)
    return jnp.asarray(squeeze), jnp.asarray(spread)


def roll(value, by):
    by = by % LANES
    return value if by == 0 else pltpu.roll(value, by, value.ndim - 1)


def lane_ids(rows):
    return lax.broadcasted_iota(jnp.int32, (rows, LANES), 1)


def split(value):
    high = value.astype(jnp.bfloat16)
    return high, (value - high.astype(jnp.float32)).astype(jnp.bfloat16)


def turn(load, r):
    return [[roll(load(f, r, SUB, t), HALF) for t in range(TILES)] for f in along_x]


def x_slope(own, other, xc_ref):
    sums = [[], []]
    for kind in range(2):
        sources = []
        for s in range(2):
            if kind == 0:
                sources.append((own[s] + other[3 - s], other[s] + own[3 - s]))
            else:
                sources.append((own[s] - other[3 - s], other[s] - own[3 - s]))
        for t in range(2):
            total = None
            for s in range(2):
                for swap in range(2):
                    term = sources[s][swap] * xc_ref[((kind * 2 + t) * 2 + s) * 2 + swap]
                    total = term if total is None else total + term
            sums[kind].append(total)
    slopes = [None] * TILES
    for t in range(2):
        even, odd = sums[0][t], sums[1][t]
        slopes[t] = even + odd
        slopes[3 - t] = roll(odd - even, HALF)
    return slopes


def begin_operator(split_rows, tabs, first, rows):
    w1_ref, w2_ref, _ = tabs
    left, right = [], []
    for r in range(first, first + rows, PACK):
        for t in range(TILES):
            parts = {f: split_rows(f, r, PACK, t) for f in both_yz + pairs_yz[0] + pairs_yz[1]}
            for f in both_yz:
                high, low = parts[f]
                left.append(jnp.concatenate([high, low, high], 1))
            for f, g in pairs_yz:
                (high_f, low_f), (high_g, low_g) = parts[f], parts[g]
                right.append(jnp.concatenate([high_f, high_g, low_f, low_g, high_f, high_g], 1))
    left, right = jnp.concatenate(left, 0), jnp.concatenate(right, 0)
    return (
        jnp.dot(left, w1_ref[...], preferred_element_type=jnp.float32),
        jnp.dot(right, w2_ref[...], preferred_element_type=jnp.float32),
    )


def end_operator(load, material, tabs, products, first, rows, scale, emit):
    xc_ref = tabs[2]
    o1, o2 = products

    def yz(values, count, i, t, r):
        at = (((r - first) // PACK * TILES + t) * count + i) * PACK + r % PACK
        return values[at : at + SUB, :LANES], values[at : at + SUB, LANES:]

    following = turn(load, first)
    for r in range(first, first + rows, SUB):
        turned = following
        if r + SUB < first + rows:
            following = turn(load, r + SUB)
        slopes = [
            x_slope([load(f, r, SUB, t) for t in range(TILES)], turned[i], xc_ref) for i, f in enumerate(along_x)
        ]
        factor = scale(r)
        for t in range(TILES):
            lame, shear, light = [m if factor is None else m * factor for m in material(r, t)]
            shear_2 = shear + shear
            dy_vx, dz_vx = yz(o1, 4, 0, t, r)
            dy_vy, dz_vy = yz(o1, 4, 1, t, r)
            dy_vz, dz_vz = yz(o1, 4, 2, t, r)
            dy_syz, dz_syz = yz(o1, 4, 3, t, r)
            dy_syy, dz_szz = yz(o2, 2, 0, t, r)
            dy_sxy, dz_sxz = yz(o2, 2, 1, t, r)
            dx_vx, dx_vy, dx_vz, dx_sxx, dx_sxy, dx_sxz = (slope[t] for slope in slopes)
            diverge = lame * (dx_vx + dy_vy + dz_vz)
            emit(0, r, t, diverge + shear_2 * dx_vx)
            emit(1, r, t, diverge + shear_2 * dy_vy)
            emit(2, r, t, diverge + shear_2 * dz_vz)
            emit(3, r, t, shear * (dy_vx + dx_vy))
            emit(4, r, t, shear * (dz_vy + dy_vz))
            emit(5, r, t, shear * (dz_vx + dx_vz))
            emit(6, r, t, light * (dx_sxx + dy_sxy + dz_sxz))
            emit(7, r, t, light * (dx_sxy + dy_syy + dz_syz))
            emit(8, r, t, light * (dx_sxz + dy_syz + dz_szz))


def apply_operator(load, split_rows, material, tabs, rows, size, scale, emit):
    groups = range(0, rows, size)
    products = [begin_operator(split_rows, tabs, first, size) for first in groups]
    for first, product in zip(groups, products):
        end_operator(load, material, tabs, product, first, size, scale, emit)


def span(tile):
    return slice(tile * LANES, (tile + 1) * LANES)


def pack_faces(read, rows):
    low = lane_ids(rows // 2) < HALF
    first, second = read(0, 0), read(rows // 2, 0)
    start = jnp.where(low, first, roll(second, HALF))
    first, second = read(0, 3), read(rows // 2, 3)
    end = jnp.where(low, roll(first, HALF), second)
    return end, start


def odd_device():
    return lax.rem(lax.axis_index("space"), 2) == 1


def send_faces(odd, near_ref, far_ref, index, end, start):
    near_ref[index] = jnp.where(odd, end, start)
    far_ref[index] = jnp.where(odd, start, end)


def got_faces(odd, near_ref, far_ref, index):
    near, far = near_ref[index], far_ref[index]
    return jnp.where(odd, far, near), jnp.where(odd, near, far)


def wave_speed(density, lame, shear):
    return jnp.sqrt((lame + 2.0 * shear) / density)


def early_kernel(*refs):
    sources, targets = refs[:LOADED], refs[LOADED : 2 * LOADED]
    out_ref, far_ref, near_ref = refs[2 * LOADED : 2 * LOADED + 3]
    sems = refs[2 * LOADED + 3]
    sol_ref, mat_ref, w1_ref, w2_ref, xc_ref = targets[:5]
    rows = out_ref.shape[1]
    upper, lower = pl.ds(rows, rows), pl.ds(0, rows)
    pairs = [(sources[i].at[:, upper, :], targets[i].at[:, upper, :]) for i in range(2)]
    pairs += [(sources[i], targets[i]) for i in range(2, 5)]
    pairs += [(sources[i].at[:, lower, :], targets[i].at[:, lower, :]) for i in range(2)]
    pairs += [(sources[i], targets[i]) for i in range(5, LOADED)]
    copies = [pltpu.make_async_copy(source, target, sems.at[i]) for i, (source, target) in enumerate(pairs)]
    for copy in copies:
        copy.start()
    for copy in copies[:5]:
        copy.wait()
    load = lambda f, r, count, t: sol_ref[f, rows + r : rows + r + count, span(t)]
    material = lambda r, t: (
        mat_ref[1, rows + r : rows + r + SUB, span(t)],
        mat_ref[2, rows + r : rows + r + SUB, span(t)],
        1.0 / mat_ref[0, rows + r : rows + r + SUB, span(t)],
    )

    def emit(f, r, t, value):
        base = time_step * load(f, r, SUB, t)
        out_ref[f, r : r + SUB, span(t)] = base + value

    split_rows = lambda f, r, count, t: split(load(f, r, count, t))
    tabs = (w1_ref, w2_ref, xc_ref)
    apply_operator(load, split_rows, material, tabs, rows, rows // 2, lambda r: taylor_weight(1), emit)
    for copy in copies[5:]:
        copy.wait()
    count = rows // 2
    odd = odd_device()
    for f in range(9):
        end, start = pack_faces(lambda r, t, f=f: out_ref[f, r : r + count, span(t)], rows)
        send_faces(odd, near_ref, far_ref, f, end, start)
    for i in range(2):

        def speed(r, t, i=i):
            return wave_speed(*[mat_ref[m, i * rows + r : i * rows + r + count, span(t)] for m in range(3)])

        end, start = pack_faces(speed, rows)
        send_faces(odd, near_ref, far_ref, 9 + i, end, start)


def refined_kernel(
    count_ref, sol_ref, mat_ref, w1_ref, w2_ref, xc_ref, squeeze_hbm, spread_hbm,
    out_ref, far_ref, near_ref, squeeze_ref, spread_ref, state, light, sems,
):
    loads = [
        pltpu.make_async_copy(squeeze_hbm, squeeze_ref, sems.at[0]),
        pltpu.make_async_copy(spread_hbm, spread_ref, sems.at[1]),
    ]
    for copy in loads:
        copy.start()
    rows = out_ref.shape[1]
    limit = count_ref[0, 0]
    light[...] = 1.0 / mat_ref[0, :rows, :]
    tabs = (w1_ref, w2_ref, xc_ref)
    material = lambda r, t: (
        mat_ref[1, r : r + SUB, span(t)],
        mat_ref[2, r : r + SUB, span(t)],
        light[r : r + SUB, span(t)],
    )

    def next_term(source, scale, first, used):
        load = lambda f, r, count, t: source[f, r : r + count, span(t)]
        split_rows = lambda f, r, count, t: split(load(f, r, count, t))

        def emit(f, r, t, value):
            at = pl.ds(r, SUB)
            before = time_step * sol_ref[f, at, span(t)] if first else out_ref[f, at, span(t)]
            state[f, at, span(t)] = value
            out_ref[f, at, span(t)] = before + value

        apply_operator(load, split_rows, material, tabs, used, rows // 2, scale, emit)

    def term(used, degree, carry):
        ratio = time_step / jnp.full((SUB, LANES), degree + 1, jnp.int32).astype(jnp.float32)

        def scale(r):
            ids = r + lax.broadcasted_iota(jnp.int32, (SUB, LANES), 0)
            return jnp.where(ids < limit, ratio, 0.0)

        next_term(state, scale, False, used)
        return carry

    next_term(sol_ref, lambda r: taylor_weight(1), True, rows)

    @pl.when(limit > rows // 2)
    def _():
        lax.fori_loop(2, ORD, functools.partial(term, rows), 0)

    @pl.when(limit <= rows // 2)
    def _():
        lax.fori_loop(2, ORD, functools.partial(term, rows // 2), 0)

    for copy in loads:
        copy.wait()
    count = rows // 2
    odd = odd_device()
    for f in range(9):
        end, start = pack_faces(lambda r, t, f=f: out_ref[f, r : r + count, span(t)], rows)
        send_faces(odd, near_ref, far_ref, f, end, start)


def hot(row, first, count):
    cells = row.shape[1]
    ids = first + lax.broadcasted_iota(jnp.int32, (count, cells), 0)
    return jnp.where(ids == row, 1.0, 0.0).T


def hot_back(row):
    cells = row.shape[1]
    ids = lax.broadcasted_iota(jnp.int32, (cells, cells), 0)
    return jnp.where(ids == row, 1.0, 0.0).astype(jnp.bfloat16)


def unpack_faces(after, before):
    low = lane_ids(after.shape[0]) < HALF
    return jnp.concatenate(
        [
            jnp.where(low, after, 0.0),
            jnp.where(low, roll(after, HALF), 0.0),
            jnp.where(low, 0.0, roll(before, HALF)),
            jnp.where(low, 0.0, before),
        ],
        0,
    )


def flux(direction, jump, lame, shear, light, speed):
    members = ((6, 7, 8, 0, 3, 5), (6, 7, 8, 3, 1, 4), (6, 7, 8, 5, 4, 2))[direction]
    g = [jump[m] for m in members]
    through = g[direction]
    spread_out = lame * through
    normal = [spread_out, spread_out, spread_out, None, None, None, light * g[3], light * g[4], light * g[5]]
    normal[direction] = spread_out + 2.0 * (shear * through)
    if direction == 0:
        normal[3], normal[5] = shear * g[1], shear * g[2]
    elif direction == 1:
        normal[3], normal[4] = shear * g[0], shear * g[2]
    else:
        normal[4], normal[5] = shear * g[1], shear * g[0]
    return [
        speed * jump[f] if normal[f] is None else normal[f] + speed * jump[f] for f in range(9)
    ]


def correct_kernel(
    sol_ref, mat_ref, low_ref, high_ref, beside_ref, far_ref, near_ref,
    w1_ref, w2_ref, xc_ref, squeeze_ref, spread_ref,
    out_ref, ends_ref, xmat_ref, late_ref,
    pieces, compact, xfix, hot_ref, rhs, far, fix, fixed, light, fixes, middle, sems,
):
    cells = sol_ref.shape[1]
    half = low_ref.shape[1]
    nodes = sol_ref.shape[2]
    in_low = lane_ids(SUB) < HALF
    all_low = lane_ids(cells) < HALF
    in_first = lane_ids(cells) % HALF < HALF // 2
    side = jnp.where(in_low, 0.25, -0.25)

    def integral(f, r, count, t):
        if r < half:
            return low_ref[f, r : r + count, span(t)]
        return high_ref[f, r - half : r - half + count, span(t)]

    for f in range(12):
        for start in (0, half):
            at = pl.ds(f * cells + start, half)
            for t in range(TILES):
                value = integral(f, start, half, t) if f < 9 else mat_ref[f - 9, start : start + half, span(t)]
                high, low = split(value)
                pieces[at, span(t)] = high
                pieces[at, nodes + t * LANES : nodes + (t + 1) * LANES] = low
    for f in range(0, 12, 3):
        at = pl.ds(f * cells, 3 * cells)
        compact[at, :] = jnp.dot(pieces[at, :], squeeze_ref[...], preferred_element_type=jnp.float32)
    light[...] = 1.0 / mat_ref[0]

    here = beside_ref[...] % cells
    odd = odd_device()
    for k in range(2):
        direction = k + 1
        plus = hot_back(here[2 * direction : 2 * direction + 1])
        minus = hot_back(here[2 * direction + 1 : 2 * direction + 2])
        for i in range(2):
            hot_ref[k, :, 2 * i * LANES : (2 * i + 1) * LANES] = plus
            hot_ref[k, :, (2 * i + 1) * LANES : (2 * i + 2) * LANES] = minus

        def face(f, k=k):
            return compact[pl.ds(f * cells, cells), span(k)]

        for f in range(10):
            own = face(f) if f < 9 else wave_speed(face(9), face(10), face(11))
            if f == 9:
                far[k, :, span(10)] = own
            turned = roll(own, HALF)
            for i, piece in enumerate((jnp.where(all_low, turned, 0.0), jnp.where(all_low, 0.0, turned))):
                high, low = split(piece)
                rhs[k, i * LANES : (i + 1) * LANES, span(f)] = high
                rhs[k, (i + 2) * LANES : (i + 3) * LANES, span(f)] = low
        far[k, :, : 10 * LANES] = jnp.dot(hot_ref[k], rhs[k], preferred_element_type=jnp.float32)
        for r in range(0, cells, SUB):
            at = pl.ds(r, SUB)

            def own(f, k=k, r=r):
                return compact[pl.ds(f * cells + r, SUB), span(k)]

            jump = [far[k, at, span(f)] - own(f) for f in range(9)]
            speed = 0.25 * jnp.maximum(far[k, at, span(9)], far[k, at, span(10)])
            values = flux(direction, jump, side * own(10), side * own(11), side / own(9), speed)
            for f, value in enumerate(values):
                fix[pl.ds(f * cells + r, SUB), span(k)] = value
    for f in range(9):
        at = pl.ds(f * cells, cells)
        along, across = fix[at, span(0)], fix[at, span(1)]
        for k, value in enumerate((jnp.where(in_first, along, across), jnp.where(in_first, across, along))):
            high, low = split(value)
            fixed[at, span(2 * k)] = high
            fixed[at, span(2 * k + 1)] = low

    plus, minus = here[1:2], here[0:1]
    plus, minus = hot(plus, 0, cells), hot(minus, 0, cells)
    early = jnp.concatenate([plus[:, half:], minus[:, half:]], 1).astype(jnp.bfloat16)
    late = jnp.concatenate([plus[:, :half], minus[:, :half]], 1).astype(jnp.bfloat16)
    late_ref[:, :LANES] = late
    late_ref[:, LANES:] = late
    hot_ref[2, :, 0 * LANES : 1 * LANES] = early
    hot_ref[2, :, 1 * LANES : 2 * LANES] = early
    hot_ref[2, :, 2 * LANES : 3 * LANES] = late
    hot_ref[2, :, 3 * LANES : 4 * LANES] = late
    for f in range(9):
        high, low = split(unpack_faces(*got_faces(odd, near_ref, far_ref, f)))
        rhs[2, 0:LANES, span(f)] = high
        rhs[2, LANES : 2 * LANES, span(f)] = low
    for k, f in ((0, 10), (2, 9)):
        high, low = split(unpack_faces(*got_faces(odd, near_ref, far_ref, f)))
        rhs[2, k * LANES : (k + 1) * LANES, span(9)] = high
        rhs[2, (k + 1) * LANES : (k + 2) * LANES, span(9)] = low
    far[2, :, : 9 * LANES] = jnp.dot(
        hot_ref[2, :, : 2 * LANES], rhs[2, : 2 * LANES, : 9 * LANES], preferred_element_type=jnp.float32
    )
    far[2, :, span(9)] = jnp.dot(hot_ref[2], rhs[2, :, span(9)], preferred_element_type=jnp.float32)
    for r in range(0, cells, SUB):
        at = pl.ds(r, SUB)
        jump = [
            far[2, at, span(f)] - jnp.where(in_low, integral(f, r, SUB, 0), integral(f, r, SUB, 3)) for f in range(9)
        ]
        density, lame, shear = (
            jnp.where(in_low, mat_ref[m, at, span(0)], mat_ref[m, at, span(3)]) for m in range(3)
        )
        speed = 0.25 * jnp.maximum(far[2, at, span(9)], wave_speed(density, lame, shear))
        lame, shear, weight = side * lame, side * shear, side / density
        for f, value in enumerate(flux(0, jump, lame, shear, weight, speed)):
            xfix[f, at, :] = value
        for i, value in enumerate((lame, shear, weight, speed)):
            xmat_ref[i, at, :] = value

    for k in range(2):
        at = slice(2 * k * LANES, 2 * (k + 1) * LANES)
        fixes[:, at] = jnp.dot(fixed[:, at], spread_ref[at, :], preferred_element_type=jnp.float32)

    def split_rows(f, r, count, t):
        at = pl.ds(f * cells + r, count)
        return pieces[at, span(t)], pieces[at, nodes + t * LANES : nodes + (t + 1) * LANES]

    def material(r, t):
        at = pl.ds(r, SUB)
        return mat_ref[1, at, span(t)], mat_ref[2, at, span(t)], light[at, span(t)]

    def emit(f, r, t, value):
        at = pl.ds(r, SUB)
        total = sol_ref[f, at, span(t)] + value + fixes[pl.ds(f * cells + r, SUB), span(t)]
        if t == 0:
            ends_ref[0, f, at, :] = total + jnp.where(in_low, xfix[f, at, :], 0.0)
        elif t == TILES - 1:
            ends_ref[1, f, at, :] = total + jnp.where(in_low, 0.0, xfix[f, at, :])
        else:
            middle[f, at, span(t - 1)] = total
        if f == 8 and t == TILES - 1 and (r + SUB) % half == 0:
            stores[r // half].start()

    between = pl.ds(LANES, (TILES - 2) * LANES)
    stores = [
        pltpu.make_async_copy(
            middle.at[:, pl.ds(start, half), :], out_ref.at[:, pl.ds(start, half), between], sems.at[i]
        )
        for i, start in enumerate(range(0, cells, half))
    ]
    tabs = (w1_ref, w2_ref, xc_ref)
    apply_operator(integral, split_rows, material, tabs, cells, half, lambda r: None, emit)
    for copy in stores:
        copy.wait()


def finish_kernel(done_ref, ends_ref, far_ref, near_ref, xmat_ref, late_ref, out_ref, ends, rhs, far, sems):
    del done_ref
    cells = ends.shape[2]
    odd = odd_device()
    for f in range(9):
        high, low = split(unpack_faces(*got_faces(odd, near_ref, far_ref, f)))
        rhs[0:LANES, span(f)] = high
        rhs[LANES : 2 * LANES, span(f)] = low
    for f in range(0, 9, 3):
        columns = slice(f * LANES, (f + 3) * LANES)
        far[:, columns] = jnp.dot(late_ref[...], rhs[:, columns], preferred_element_type=jnp.float32)
    in_low = lane_ids(SUB) < HALF
    size = cells // sems.shape[1]
    stores = []
    for r in range(0, cells, SUB):
        at = pl.ds(r, SUB)
        jump = [far[at, span(f)] for f in range(9)]
        lame, shear, weight, speed = (xmat_ref[i, at, :] for i in range(4))
        for f, value in enumerate(flux(0, jump, lame, shear, weight, speed)):
            ends[0, f, at, :] = ends_ref[0, f, at, :] + jnp.where(in_low, value, 0.0)
            ends[1, f, at, :] = ends_ref[1, f, at, :] + jnp.where(in_low, 0.0, value)
        if (r + SUB) % size == 0:
            part = pl.ds(r + SUB - size, size)
            for i, t in enumerate((0, TILES - 1)):
                copy = pltpu.make_async_copy(
                    ends.at[i, :, part, :], out_ref.at[:, part, pl.ds(t * LANES, LANES)], sems.at[i, r // size]
                )
                copy.start()
                stores.append(copy)
    for copy in stores:
        copy.wait()


def exchange(near, far):
    peers = lax.axis_size("space")
    got_near = lax.ppermute(near, "space", [(i, i + (-1 if i % 2 else 1)) for i in range(peers)])
    got_far = lax.ppermute(far, "space", [(i, (i + (1 if i % 2 else -1)) % peers) for i in range(peers)])
    return got_near, got_far


def f32(*shape):
    return jax.ShapeDtypeStruct(shape, jnp.float32)


def on_device(solution, material, neighbours, refine_count):
    cells, nodes = solution.shape[1:]
    rows = REF_MAX
    params = lambda mib: pltpu.CompilerParams(vmem_limit_bytes=mib * 1024 * 1024)
    early_shape, late_shape = (11, rows // 2, LANES), (9, rows // 2, LANES)
    in_vmem = pl.BlockSpec(memory_space=pltpu.VMEM)
    in_hbm = pl.BlockSpec(memory_space=pltpu.HBM)

    sources = (solution, material) + tables()
    pinned = lambda arrays: [pltpu.with_memory_space_constraint(x, pltpu.HBM) for x in arrays]
    faces = face_tables()
    *loaded, high, far, near = pl.pallas_call(
        early_kernel,
        in_specs=[in_hbm] * LOADED,
        out_specs=[in_vmem] * (LOADED + 3),
        out_shape=[pltpu.VMEM(x.shape, x.dtype) for x in sources]
        + [pltpu.VMEM((9, rows, nodes), jnp.float32), f32(*early_shape), f32(*early_shape)],
        scratch_shapes=[pltpu.SemaphoreType.DMA((LOADED + 2,))],
        compiler_params=params(20),
        name="early",
    )(*pinned(sources))
    sol, mat, w1, w2, xc = loaded
    early_near, early_far = exchange(near, far)

    low, far, near, squeeze, spread = pl.pallas_call(
        refined_kernel,
        in_specs=[pl.BlockSpec(memory_space=pltpu.SMEM)] + [in_vmem] * 5 + [in_hbm] * 2,
        out_specs=[in_vmem] * 5,
        out_shape=[pltpu.VMEM((9, rows, nodes), jnp.float32), f32(*late_shape), f32(*late_shape)]
        + [pltpu.VMEM(x.shape, x.dtype) for x in faces],
        scratch_shapes=[
            pltpu.VMEM((9, rows, nodes), jnp.float32),
            pltpu.VMEM((rows, nodes), jnp.float32),
            pltpu.SemaphoreType.DMA((2,)),
        ],
        compiler_params=params(20),
        name="refined",
    )(refine_count, sol, mat, w1, w2, xc, *pinned(faces))
    late_near, late_far = exchange(near, far)

    done, ends, xmat, late_hot = pl.pallas_call(
        correct_kernel,
        in_specs=[in_vmem] * 12,
        out_specs=[in_hbm] + [in_vmem] * 3,
        out_shape=[
            pltpu.HBM(solution.shape, jnp.float32),
            pltpu.VMEM((2, 9, cells, LANES), jnp.float32),
            pltpu.VMEM((4, cells, LANES), jnp.float32),
            pltpu.VMEM((cells, 2 * LANES), jnp.bfloat16),
        ],
        scratch_shapes=[
            pltpu.VMEM((12 * cells, 2 * nodes), jnp.bfloat16),
            pltpu.VMEM((12 * cells, 2 * LANES), jnp.float32),
            pltpu.VMEM((9, cells, LANES), jnp.float32),
            pltpu.VMEM((3, cells, 4 * LANES), jnp.bfloat16),
            pltpu.VMEM((3, 4 * LANES, 10 * LANES), jnp.bfloat16),
            pltpu.VMEM((3, cells, 11 * LANES), jnp.float32),
            pltpu.VMEM((9 * cells, 2 * LANES), jnp.float32),
            pltpu.VMEM((9 * cells, 4 * LANES), jnp.bfloat16),
            pltpu.VMEM((cells, nodes), jnp.float32),
            pltpu.VMEM((9 * cells, nodes), jnp.float32),
            pltpu.VMEM((9, cells, nodes - 2 * LANES), jnp.float32),
            pltpu.SemaphoreType.DMA((2,)),
        ],
        compiler_params=params(40),
        name="correct",
    )(sol, mat, low, high, neighbours, early_far, early_near, w1, w2, xc, squeeze, spread)

    return pl.pallas_call(
        finish_kernel,
        in_specs=[in_hbm] + [in_vmem] * 5,
        out_specs=in_hbm,
        out_shape=f32(*solution.shape),
        scratch_shapes=[
            pltpu.VMEM((2, 9, cells, LANES), jnp.float32),
            pltpu.VMEM((2 * LANES, 9 * LANES), jnp.bfloat16),
            pltpu.VMEM((cells, 9 * LANES), jnp.float32),
            pltpu.SemaphoreType.DMA((2, 4)),
        ],
        input_output_aliases={0: 0},
        compiler_params=params(8),
        name="finish",
    )(done, ends, late_far, late_near, xmat, late_hot)


def solution(mesh):
    in_specs = (
        P(None, ("space", "help"), None),
        P(None, ("space", "help"), None),
        P(None, ("space", "help")),
        P("space", "help"),
    )
    out_specs = P(None, ("space", "help"), None)
    return jax.shard_map(
        on_device, mesh=mesh, in_specs=in_specs, out_specs=out_specs, check_vma=False
    )
```

```python
import functools
import math

import jax
import jax.numpy as jnp
import ml_dtypes
import numpy as np
from jax import lax
from jax.experimental import pallas as pl
from jax.experimental.pallas import tpu as pltpu
from jax.sharding import PartitionSpec as P

P_SIZE = 8
ORD = 8
REF_MAX = 64
LANES = 128
TILES = 4
HALF = 64
SUB = 8
PACK = 16
LOADED = 5

along_x = (6, 7, 8, 0, 3, 5)
along_y = (6, 7, 8, 3, 1, 4)
along_z = (6, 7, 8, 5, 4, 2)
both_yz = (6, 7, 8, 4)
pairs_yz = ((1, 2), (3, 5))
time_step = 0.5


def cheb_table(node_count):
    intervals = node_count - 1
    places = np.arange(node_count)
    points = np.cos(np.pi * places / intervals)
    weights = np.where((places == 0) | (places == intervals), 2.0, 1.0)
    scaled = weights * (-1.0) ** places
    differ = points[:, None] - points[None, :] + np.eye(node_count)
    matrix = np.outer(scaled, 1.0 / scaled) / differ
    matrix = matrix - np.eye(node_count) * np.sum(matrix, axis=1)[:, None]
    return matrix / (node_count * node_count / 4.0)


def taylor_weight(degree):
    return time_step ** (degree + 1) / math.factorial(degree + 1)


def tables():
    slope = cheb_table(P_SIZE).astype(np.float32).astype(np.float64)
    high = slope.astype(ml_dtypes.bfloat16).astype(np.float64)
    low = slope - high
    one = np.eye(P_SIZE)
    two = np.eye(2)

    def spread(matrix):
        along_b = np.kron(two, np.kron(matrix.T, one))
        along_e = np.kron(two, np.kron(one, matrix.T))
        return along_b, along_e

    hy, hz = spread(high)
    ly, lz = spread(low)
    none = np.zeros_like(hy)
    w1 = np.concatenate(
        [np.concatenate([hy, hz], 1), np.concatenate([hy, hz], 1), np.concatenate([ly, lz], 1)], 0
    )
    diag_high = np.block([[hy, none], [none, hz]])
    diag_low = np.block([[ly, none], [none, lz]])
    w2 = np.concatenate([diag_high, diag_high, diag_low], 0)

    half = P_SIZE // 2
    top = slope[:half, :half]
    mirror = slope[:half, ::-1][:, :half]
    lane_half = np.arange(LANES) // HALF
    rows = []
    for part in ((top + mirror) / 2, (top - mirror) / 2):
        for t in range(2):
            for s in range(2):
                for source in (lane_half, 1 - lane_half):
                    rows.append(part[2 * t + lane_half, 2 * s + source])
    xc = np.broadcast_to(np.stack(rows)[:, None, :], (len(rows), SUB, LANES))
    return (
        jnp.asarray(w1.astype(ml_dtypes.bfloat16)),
        jnp.asarray(w2.astype(ml_dtypes.bfloat16)),
        jnp.asarray(np.ascontiguousarray(xc).astype(np.float32)),
    )


def face_tables():
    node = np.arange(P_SIZE**3)
    places = (node // P_SIZE % P_SIZE, node % P_SIZE)
    others = (
        node // HALF * P_SIZE + node % P_SIZE,
        (node // HALF + P_SIZE // 2) % P_SIZE * P_SIZE + node // P_SIZE % P_SIZE,
    )
    pick = np.zeros((P_SIZE**3, 2 * LANES))
    for k in range(2):
        for side, place in enumerate((0, P_SIZE - 1)):
            on = places[k] == place
            pick[node[on], k * LANES + side * HALF + others[k][on]] = 1.0
    squeeze = np.concatenate([pick, pick], 0).astype(ml_dtypes.bfloat16)
    in_first = np.arange(LANES) % HALF < HALF // 2
    both = []
    for part in range(2):
        keep_y = in_first if part == 0 else ~in_first
        mixed = np.where(keep_y[None, :], pick[:, :LANES], pick[:, LANES:])
        piece = mixed[part * 2 * LANES : (part + 1) * 2 * LANES].T
        both += [piece, piece]
    spread = np.concatenate(both, 0).astype(ml_dtypes.bfloat16)
    return jnp.asarray(squeeze), jnp.asarray(spread)


def roll(value, by):
    by = by % LANES
    return value if by == 0 else pltpu.roll(value, by, value.ndim - 1)


def lane_ids(rows):
    return lax.broadcasted_iota(jnp.int32, (rows, LANES), 1)


def split(value):
    high = value.astype(jnp.bfloat16)
    return high, (value - high.astype(jnp.float32)).astype(jnp.bfloat16)


def turn(load, r):
    return [[roll(load(f, r, SUB, t), HALF) for t in range(TILES)] for f in along_x]


def x_slope(own, other, xc_ref):
    sums = [[], []]
    for kind in range(2):
        sources = []
        for s in range(2):
            if kind == 0:
                sources.append((own[s] + other[3 - s], other[s] + own[3 - s]))
            else:
                sources.append((own[s] - other[3 - s], other[s] - own[3 - s]))
        for t in range(2):
            total = None
            for s in range(2):
                for swap in range(2):
                    term = sources[s][swap] * xc_ref[((kind * 2 + t) * 2 + s) * 2 + swap]
                    total = term if total is None else total + term
            sums[kind].append(total)
    slopes = [None] * TILES
    for t in range(2):
        even, odd = sums[0][t], sums[1][t]
        slopes[t] = even + odd
        slopes[3 - t] = roll(odd - even, HALF)
    return slopes


def begin_operator(split_rows, tabs, first, rows):
    w1_ref, w2_ref, _ = tabs
    left, right = [], []
    for r in range(first, first + rows, PACK):
        for t in range(TILES):
            parts = {f: split_rows(f, r, PACK, t) for f in both_yz + pairs_yz[0] + pairs_yz[1]}
            for f in both_yz:
                high, low = parts[f]
                left.append(jnp.concatenate([high, low, high], 1))
            for f, g in pairs_yz:
                (high_f, low_f), (high_g, low_g) = parts[f], parts[g]
                right.append(jnp.concatenate([high_f, high_g, low_f, low_g, high_f, high_g], 1))
    left, right = jnp.concatenate(left, 0), jnp.concatenate(right, 0)
    return (
        jnp.dot(left, w1_ref[...], preferred_element_type=jnp.float32),
        jnp.dot(right, w2_ref[...], preferred_element_type=jnp.float32),
    )


def end_operator(load, material, tabs, products, first, rows, scale, emit):
    xc_ref = tabs[2]
    o1, o2 = products

    def yz(values, count, i, t, r):
        at = (((r - first) // PACK * TILES + t) * count + i) * PACK + r % PACK
        return values[at : at + SUB, :LANES], values[at : at + SUB, LANES:]

    following = turn(load, first)
    for r in range(first, first + rows, SUB):
        turned = following
        if r + SUB < first + rows:
            following = turn(load, r + SUB)
        slopes = [
            x_slope([load(f, r, SUB, t) for t in range(TILES)], turned[i], xc_ref) for i, f in enumerate(along_x)
        ]
        factor = scale(r)
        for t in range(TILES):
            lame, shear, light = [m if factor is None else m * factor for m in material(r, t)]
            shear_2 = shear + shear
            dy_vx, dz_vx = yz(o1, 4, 0, t, r)
            dy_vy, dz_vy = yz(o1, 4, 1, t, r)
            dy_vz, dz_vz = yz(o1, 4, 2, t, r)
            dy_syz, dz_syz = yz(o1, 4, 3, t, r)
            dy_syy, dz_szz = yz(o2, 2, 0, t, r)
            dy_sxy, dz_sxz = yz(o2, 2, 1, t, r)
            dx_vx, dx_vy, dx_vz, dx_sxx, dx_sxy, dx_sxz = (slope[t] for slope in slopes)
            diverge = lame * (dx_vx + dy_vy + dz_vz)
            emit(0, r, t, diverge + shear_2 * dx_vx)
            emit(1, r, t, diverge + shear_2 * dy_vy)
            emit(2, r, t, diverge + shear_2 * dz_vz)
            emit(3, r, t, shear * (dy_vx + dx_vy))
            emit(4, r, t, shear * (dz_vy + dy_vz))
            emit(5, r, t, shear * (dz_vx + dx_vz))
            emit(6, r, t, light * (dx_sxx + dy_sxy + dz_sxz))
            emit(7, r, t, light * (dx_sxy + dy_syy + dz_syz))
            emit(8, r, t, light * (dx_sxz + dy_syz + dz_szz))


def apply_operator(load, split_rows, material, tabs, rows, size, scale, emit):
    groups = range(0, rows, size)
    products = [begin_operator(split_rows, tabs, first, size) for first in groups]
    for first, product in zip(groups, products):
        end_operator(load, material, tabs, product, first, size, scale, emit)


def span(tile):
    return slice(tile * LANES, (tile + 1) * LANES)


def pack_faces(read, rows):
    low = lane_ids(rows // 2) < HALF
    first, second = read(0, 0), read(rows // 2, 0)
    start = jnp.where(low, first, roll(second, HALF))
    first, second = read(0, 3), read(rows // 2, 3)
    end = jnp.where(low, roll(first, HALF), second)
    return end, start


def odd_device():
    return lax.rem(lax.axis_index("space"), 2) == 1


def send_faces(odd, near_ref, far_ref, index, end, start):
    near_ref[index] = jnp.where(odd, end, start)
    far_ref[index] = jnp.where(odd, start, end)


def got_faces(odd, near_ref, far_ref, index):
    near, far = near_ref[index], far_ref[index]
    return jnp.where(odd, far, near), jnp.where(odd, near, far)


def wave_speed(density, lame, shear):
    return jnp.sqrt((lame + 2.0 * shear) / density)


def early_kernel(*refs):
    sources, targets = refs[:LOADED], refs[LOADED : 2 * LOADED]
    out_ref, far_ref, near_ref = refs[2 * LOADED : 2 * LOADED + 3]
    sems = refs[2 * LOADED + 3]
    sol_ref, mat_ref, w1_ref, w2_ref, xc_ref = targets[:5]
    rows = out_ref.shape[1]
    upper, lower = pl.ds(rows, rows), pl.ds(0, rows)
    pairs = [(sources[i].at[:, upper, :], targets[i].at[:, upper, :]) for i in range(2)]
    pairs += [(sources[i], targets[i]) for i in range(2, 5)]
    pairs += [(sources[i].at[:, lower, :], targets[i].at[:, lower, :]) for i in range(2)]
    pairs += [(sources[i], targets[i]) for i in range(5, LOADED)]
    copies = [pltpu.make_async_copy(source, target, sems.at[i]) for i, (source, target) in enumerate(pairs)]
    for copy in copies:
        copy.start()
    for copy in copies[:5]:
        copy.wait()
    load = lambda f, r, count, t: sol_ref[f, rows + r : rows + r + count, span(t)]
    material = lambda r, t: (
        mat_ref[1, rows + r : rows + r + SUB, span(t)],
        mat_ref[2, rows + r : rows + r + SUB, span(t)],
        1.0 / mat_ref[0, rows + r : rows + r + SUB, span(t)],
    )

    def emit(f, r, t, value):
        base = time_step * load(f, r, SUB, t)
        out_ref[f, r : r + SUB, span(t)] = base + value

    split_rows = lambda f, r, count, t: split(load(f, r, count, t))
    tabs = (w1_ref, w2_ref, xc_ref)
    apply_operator(load, split_rows, material, tabs, rows, rows // 2, lambda r: taylor_weight(1), emit)
    for copy in copies[5:]:
        copy.wait()
    count = rows // 2
    odd = odd_device()
    for f in range(9):
        end, start = pack_faces(lambda r, t, f=f: out_ref[f, r : r + count, span(t)], rows)
        send_faces(odd, near_ref, far_ref, f, end, start)
    for i in range(2):

        def speed(r, t, i=i):
            return wave_speed(*[mat_ref[m, i * rows + r : i * rows + r + count, span(t)] for m in range(3)])

        end, start = pack_faces(speed, rows)
        send_faces(odd, near_ref, far_ref, 9 + i, end, start)


def refined_kernel(
    count_ref, sol_ref, mat_ref, w1_ref, w2_ref, xc_ref, squeeze_hbm, spread_hbm,
    out_ref, far_ref, near_ref, squeeze_ref, spread_ref, state, light, sems,
):
    loads = [
        pltpu.make_async_copy(squeeze_hbm, squeeze_ref, sems.at[0]),
        pltpu.make_async_copy(spread_hbm, spread_ref, sems.at[1]),
    ]
    for copy in loads:
        copy.start()
    rows = out_ref.shape[1]
    limit = count_ref[0, 0]
    light[...] = 1.0 / mat_ref[0, :rows, :]
    tabs = (w1_ref, w2_ref, xc_ref)
    material = lambda r, t: (
        mat_ref[1, r : r + SUB, span(t)],
        mat_ref[2, r : r + SUB, span(t)],
        light[r : r + SUB, span(t)],
    )

    def next_term(source, scale, first, used):
        load = lambda f, r, count, t: source[f, r : r + count, span(t)]
        split_rows = lambda f, r, count, t: split(load(f, r, count, t))

        def emit(f, r, t, value):
            at = pl.ds(r, SUB)
            before = time_step * sol_ref[f, at, span(t)] if first else out_ref[f, at, span(t)]
            state[f, at, span(t)] = value
            out_ref[f, at, span(t)] = before + value

        apply_operator(load, split_rows, material, tabs, used, rows // 2, scale, emit)

    def term(used, degree, carry):
        ratio = time_step / jnp.full((SUB, LANES), degree + 1, jnp.int32).astype(jnp.float32)

        def scale(r):
            ids = r + lax.broadcasted_iota(jnp.int32, (SUB, LANES), 0)
            return jnp.where(ids < limit, ratio, 0.0)

        next_term(state, scale, False, used)
        return carry

    next_term(sol_ref, lambda r: taylor_weight(1), True, rows)

    @pl.when(limit > rows // 2)
    def _():
        lax.fori_loop(2, ORD, functools.partial(term, rows), 0)

    @pl.when(limit <= rows // 2)
    def _():
        lax.fori_loop(2, ORD, functools.partial(term, rows // 2), 0)

    for copy in loads:
        copy.wait()
    count = rows // 2
    odd = odd_device()
    for f in range(9):
        end, start = pack_faces(lambda r, t, f=f: out_ref[f, r : r + count, span(t)], rows)
        send_faces(odd, near_ref, far_ref, f, end, start)


def hot(row, first, count):
    cells = row.shape[1]
    ids = first + lax.broadcasted_iota(jnp.int32, (count, cells), 0)
    return jnp.where(ids == row, 1.0, 0.0).T


def hot_back(row):
    cells = row.shape[1]
    ids = lax.broadcasted_iota(jnp.int32, (cells, cells), 0)
    return jnp.where(ids == row, 1.0, 0.0).astype(jnp.bfloat16)


def unpack_faces(after, before):
    low = lane_ids(after.shape[0]) < HALF
    return jnp.concatenate(
        [
            jnp.where(low, after, 0.0),
            jnp.where(low, roll(after, HALF), 0.0),
            jnp.where(low, 0.0, roll(before, HALF)),
            jnp.where(low, 0.0, before),
        ],
        0,
    )


def flux(direction, jump, lame, shear, light, speed):
    members = ((6, 7, 8, 0, 3, 5), (6, 7, 8, 3, 1, 4), (6, 7, 8, 5, 4, 2))[direction]
    g = [jump[m] for m in members]
    through = g[direction]
    spread_out = lame * through
    normal = [spread_out, spread_out, spread_out, None, None, None, light * g[3], light * g[4], light * g[5]]
    normal[direction] = spread_out + 2.0 * (shear * through)
    if direction == 0:
        normal[3], normal[5] = shear * g[1], shear * g[2]
    elif direction == 1:
        normal[3], normal[4] = shear * g[0], shear * g[2]
    else:
        normal[4], normal[5] = shear * g[1], shear * g[0]
    return [
        speed * jump[f] if normal[f] is None else normal[f] + speed * jump[f] for f in range(9)
    ]


def correct_kernel(
    sol_ref, mat_ref, low_ref, high_ref, beside_ref, far_ref, near_ref,
    w1_ref, w2_ref, xc_ref, squeeze_ref, spread_ref,
    out_ref, ends_ref, xmat_ref, late_ref,
    pieces, compact, xfix, hot_ref, xhot, rhs, far, fix, fixed, light, fixes, middle, sems,
):
    cells = sol_ref.shape[1]
    half = low_ref.shape[1]
    nodes = sol_ref.shape[2]
    in_low = lane_ids(SUB) < HALF
    in_first = lane_ids(cells) % HALF < HALF // 2
    side = jnp.where(in_low, 0.25, -0.25)

    def integral(f, r, count, t):
        if r < half:
            return low_ref[f, r : r + count, span(t)]
        return high_ref[f, r - half : r - half + count, span(t)]

    for f in range(12):
        for start in (0, half):
            at = pl.ds(f * cells + start, half)
            for t in range(TILES):
                value = integral(f, start, half, t) if f < 9 else mat_ref[f - 9, start : start + half, span(t)]
                high, low = split(value)
                pieces[at, span(t)] = high
                pieces[at, nodes + t * LANES : nodes + (t + 1) * LANES] = low
    for f in range(0, 12, 3):
        at = pl.ds(f * cells, 3 * cells)
        compact[at, :] = jnp.dot(pieces[at, :], squeeze_ref[...], preferred_element_type=jnp.float32)
    light[...] = 1.0 / mat_ref[0]

    here = beside_ref[...] % cells
    odd = odd_device()
    for k in range(2):
        direction = k + 1
        plus = hot_back(here[2 * direction : 2 * direction + 1])
        minus = hot_back(here[2 * direction + 1 : 2 * direction + 2])
        for i, pick in enumerate((plus, minus)):
            at = pl.ds(i * cells, cells)
            hot_ref[k, at, :LANES] = pick
            hot_ref[k, at, LANES:] = pick

        def face(f, k=k):
            return compact[pl.ds(f * cells, cells), span(k)]

        for f in range(10):
            own = face(f) if f < 9 else wave_speed(face(9), face(10), face(11))
            if f == 9:
                far[k, :cells, span(10)] = own
            high, low = split(roll(own, HALF))
            rhs[k, :LANES, span(f)] = high
            rhs[k, LANES : 2 * LANES, span(f)] = low
        far[k, :, : 10 * LANES] = jnp.dot(
            hot_ref[k], rhs[k, : 2 * LANES, :], preferred_element_type=jnp.float32
        )
        for r in range(0, cells, SUB):
            at = pl.ds(r, SUB)

            def own(f, k=k, r=r):
                return compact[pl.ds(f * cells + r, SUB), span(k)]

            def across(f, k=k, r=r):
                return jnp.where(in_low, far[k, pl.ds(r, SUB), span(f)], far[k, pl.ds(cells + r, SUB), span(f)])

            jump = [across(f) - own(f) for f in range(9)]
            speed = 0.25 * jnp.maximum(across(9), far[k, at, span(10)])
            values = flux(direction, jump, side * own(10), side * own(11), side / own(9), speed)
            for f, value in enumerate(values):
                fix[pl.ds(f * cells + r, SUB), span(k)] = value
    for f in range(9):
        at = pl.ds(f * cells, cells)
        along, across = fix[at, span(0)], fix[at, span(1)]
        for k, value in enumerate((jnp.where(in_first, along, across), jnp.where(in_first, across, along))):
            high, low = split(value)
            fixed[at, span(2 * k)] = high
            fixed[at, span(2 * k + 1)] = low

    plus, minus = here[1:2], here[0:1]
    plus, minus = hot(plus, 0, cells), hot(minus, 0, cells)
    early = jnp.concatenate([plus[:, half:], minus[:, half:]], 1).astype(jnp.bfloat16)
    late = jnp.concatenate([plus[:, :half], minus[:, :half]], 1).astype(jnp.bfloat16)
    late_ref[:, :LANES] = late
    late_ref[:, LANES:] = late
    for i, pick in enumerate((early, early, late, late)):
        xhot[:, span(i)] = pick
    for f in range(9):
        high, low = split(unpack_faces(*got_faces(odd, near_ref, far_ref, f)))
        rhs[2, 0:LANES, span(f)] = high
        rhs[2, LANES : 2 * LANES, span(f)] = low
    for k, f in ((0, 10), (2, 9)):
        high, low = split(unpack_faces(*got_faces(odd, near_ref, far_ref, f)))
        rhs[2, k * LANES : (k + 1) * LANES, span(9)] = high
        rhs[2, (k + 1) * LANES : (k + 2) * LANES, span(9)] = low
    far[2, :cells, : 9 * LANES] = jnp.dot(
        xhot[:, : 2 * LANES], rhs[2, : 2 * LANES, : 9 * LANES], preferred_element_type=jnp.float32
    )
    far[2, :cells, span(9)] = jnp.dot(xhot[...], rhs[2, :, span(9)], preferred_element_type=jnp.float32)
    for r in range(0, cells, SUB):
        at = pl.ds(r, SUB)
        jump = [
            far[2, at, span(f)] - jnp.where(in_low, integral(f, r, SUB, 0), integral(f, r, SUB, 3)) for f in range(9)
        ]
        density, lame, shear = (
            jnp.where(in_low, mat_ref[m, at, span(0)], mat_ref[m, at, span(3)]) for m in range(3)
        )
        speed = 0.25 * jnp.maximum(far[2, at, span(9)], wave_speed(density, lame, shear))
        lame, shear, weight = side * lame, side * shear, side / density
        for f, value in enumerate(flux(0, jump, lame, shear, weight, speed)):
            xfix[f, at, :] = value
        for i, value in enumerate((lame, shear, weight, speed)):
            xmat_ref[i, at, :] = value

    for k in range(2):
        at = slice(2 * k * LANES, 2 * (k + 1) * LANES)
        fixes[:, at] = jnp.dot(fixed[:, at], spread_ref[at, :], preferred_element_type=jnp.float32)

    def split_rows(f, r, count, t):
        at = pl.ds(f * cells + r, count)
        return pieces[at, span(t)], pieces[at, nodes + t * LANES : nodes + (t + 1) * LANES]

    def material(r, t):
        at = pl.ds(r, SUB)
        return mat_ref[1, at, span(t)], mat_ref[2, at, span(t)], light[at, span(t)]

    def emit(f, r, t, value):
        at = pl.ds(r, SUB)
        total = sol_ref[f, at, span(t)] + value + fixes[pl.ds(f * cells + r, SUB), span(t)]
        if t == 0:
            ends_ref[0, f, at, :] = total + jnp.where(in_low, xfix[f, at, :], 0.0)
        elif t == TILES - 1:
            ends_ref[1, f, at, :] = total + jnp.where(in_low, 0.0, xfix[f, at, :])
        else:
            middle[f, at, span(t - 1)] = total
        if f == 8 and t == TILES - 1 and (r + SUB) % half == 0:
            stores[r // half].start()

    between = pl.ds(LANES, (TILES - 2) * LANES)
    stores = [
        pltpu.make_async_copy(
            middle.at[:, pl.ds(start, half), :], out_ref.at[:, pl.ds(start, half), between], sems.at[i]
        )
        for i, start in enumerate(range(0, cells, half))
    ]
    tabs = (w1_ref, w2_ref, xc_ref)
    apply_operator(integral, split_rows, material, tabs, cells, half, lambda r: None, emit)
    for copy in stores:
        copy.wait()


def finish_kernel(done_ref, ends_ref, far_ref, near_ref, xmat_ref, late_ref, out_ref, ends, rhs, far, sems):
    del done_ref
    cells = ends.shape[2]
    odd = odd_device()
    for f in range(9):
        high, low = split(unpack_faces(*got_faces(odd, near_ref, far_ref, f)))
        rhs[0:LANES, span(f)] = high
        rhs[LANES : 2 * LANES, span(f)] = low
    for f in range(0, 9, 3):
        columns = slice(f * LANES, (f + 3) * LANES)
        far[:, columns] = jnp.dot(late_ref[...], rhs[:, columns], preferred_element_type=jnp.float32)
    in_low = lane_ids(SUB) < HALF
    size = cells // sems.shape[1]
    stores = []
    for r in range(0, cells, SUB):
        at = pl.ds(r, SUB)
        jump = [far[at, span(f)] for f in range(9)]
        lame, shear, weight, speed = (xmat_ref[i, at, :] for i in range(4))
        for f, value in enumerate(flux(0, jump, lame, shear, weight, speed)):
            ends[0, f, at, :] = ends_ref[0, f, at, :] + jnp.where(in_low, value, 0.0)
            ends[1, f, at, :] = ends_ref[1, f, at, :] + jnp.where(in_low, 0.0, value)
        if (r + SUB) % size == 0:
            part = pl.ds(r + SUB - size, size)
            for i, t in enumerate((0, TILES - 1)):
                copy = pltpu.make_async_copy(
                    ends.at[i, :, part, :], out_ref.at[:, part, pl.ds(t * LANES, LANES)], sems.at[i, r // size]
                )
                copy.start()
                stores.append(copy)
    for copy in stores:
        copy.wait()


def exchange(near, far):
    peers = lax.axis_size("space")
    got_near = lax.ppermute(near, "space", [(i, i + (-1 if i % 2 else 1)) for i in range(peers)])
    got_far = lax.ppermute(far, "space", [(i, (i + (1 if i % 2 else -1)) % peers) for i in range(peers)])
    return got_near, got_far


def f32(*shape):
    return jax.ShapeDtypeStruct(shape, jnp.float32)


def on_device(solution, material, neighbours, refine_count):
    cells, nodes = solution.shape[1:]
    rows = REF_MAX
    params = lambda mib: pltpu.CompilerParams(vmem_limit_bytes=mib * 1024 * 1024)
    early_shape, late_shape = (11, rows // 2, LANES), (9, rows // 2, LANES)
    in_vmem = pl.BlockSpec(memory_space=pltpu.VMEM)
    in_hbm = pl.BlockSpec(memory_space=pltpu.HBM)

    sources = (solution, material) + tables()
    pinned = lambda arrays: [pltpu.with_memory_space_constraint(x, pltpu.HBM) for x in arrays]
    faces = face_tables()
    *loaded, high, far, near = pl.pallas_call(
        early_kernel,
        in_specs=[in_hbm] * LOADED,
        out_specs=[in_vmem] * (LOADED + 3),
        out_shape=[pltpu.VMEM(x.shape, x.dtype) for x in sources]
        + [pltpu.VMEM((9, rows, nodes), jnp.float32), f32(*early_shape), f32(*early_shape)],
        scratch_shapes=[pltpu.SemaphoreType.DMA((LOADED + 2,))],
        compiler_params=params(20),
        name="early",
    )(*pinned(sources))
    sol, mat, w1, w2, xc = loaded
    early_near, early_far = exchange(near, far)

    low, far, near, squeeze, spread = pl.pallas_call(
        refined_kernel,
        in_specs=[pl.BlockSpec(memory_space=pltpu.SMEM)] + [in_vmem] * 5 + [in_hbm] * 2,
        out_specs=[in_vmem] * 5,
        out_shape=[pltpu.VMEM((9, rows, nodes), jnp.float32), f32(*late_shape), f32(*late_shape)]
        + [pltpu.VMEM(x.shape, x.dtype) for x in faces],
        scratch_shapes=[
            pltpu.VMEM((9, rows, nodes), jnp.float32),
            pltpu.VMEM((rows, nodes), jnp.float32),
            pltpu.SemaphoreType.DMA((2,)),
        ],
        compiler_params=params(20),
        name="refined",
    )(refine_count, sol, mat, w1, w2, xc, *pinned(faces))
    late_near, late_far = exchange(near, far)

    done, ends, xmat, late_hot = pl.pallas_call(
        correct_kernel,
        in_specs=[in_vmem] * 12,
        out_specs=[in_hbm] + [in_vmem] * 3,
        out_shape=[
            pltpu.HBM(solution.shape, jnp.float32),
            pltpu.VMEM((2, 9, cells, LANES), jnp.float32),
            pltpu.VMEM((4, cells, LANES), jnp.float32),
            pltpu.VMEM((cells, 2 * LANES), jnp.bfloat16),
        ],
        scratch_shapes=[
            pltpu.VMEM((12 * cells, 2 * nodes), jnp.bfloat16),
            pltpu.VMEM((12 * cells, 2 * LANES), jnp.float32),
            pltpu.VMEM((9, cells, LANES), jnp.float32),
            pltpu.VMEM((2, 2 * cells, 2 * LANES), jnp.bfloat16),
            pltpu.VMEM((cells, 4 * LANES), jnp.bfloat16),
            pltpu.VMEM((3, 4 * LANES, 10 * LANES), jnp.bfloat16),
            pltpu.VMEM((3, 2 * cells, 11 * LANES), jnp.float32),
            pltpu.VMEM((9 * cells, 2 * LANES), jnp.float32),
            pltpu.VMEM((9 * cells, 4 * LANES), jnp.bfloat16),
            pltpu.VMEM((cells, nodes), jnp.float32),
            pltpu.VMEM((9 * cells, nodes), jnp.float32),
            pltpu.VMEM((9, cells, nodes - 2 * LANES), jnp.float32),
            pltpu.SemaphoreType.DMA((2,)),
        ],
        compiler_params=params(40),
        name="correct",
    )(sol, mat, low, high, neighbours, early_far, early_near, w1, w2, xc, squeeze, spread)

    return pl.pallas_call(
        finish_kernel,
        in_specs=[in_hbm] + [in_vmem] * 5,
        out_specs=in_hbm,
        out_shape=f32(*solution.shape),
        scratch_shapes=[
            pltpu.VMEM((2, 9, cells, LANES), jnp.float32),
            pltpu.VMEM((2 * LANES, 9 * LANES), jnp.bfloat16),
            pltpu.VMEM((cells, 9 * LANES), jnp.float32),
            pltpu.SemaphoreType.DMA((2, 4)),
        ],
        input_output_aliases={0: 0},
        compiler_params=params(8),
        name="finish",
    )(done, ends, late_far, late_near, xmat, late_hot)


def solution(mesh):
    in_specs = (
        P(None, ("space", "help"), None),
        P(None, ("space", "help"), None),
        P(None, ("space", "help")),
        P("space", "help"),
    )
    out_specs = P(None, ("space", "help"), None)
    return jax.shard_map(
        on_device, mesh=mesh, in_specs=in_specs, out_specs=out_specs, check_vma=False
    )
```

```python
import functools
import math

import jax
import jax.numpy as jnp
import ml_dtypes
import numpy as np
from jax import lax
from jax.experimental import pallas as pl
from jax.experimental.pallas import tpu as pltpu
from jax.sharding import PartitionSpec as P

P_SIZE = 8
ORD = 8
ORD_EXACT = 6
REF_MAX = 64
LANES = 128
TILES = 4
HALF = 64
SUB = 8
PACK = 16
LOADED = 5

along_x = (6, 7, 8, 0, 3, 5)
along_y = (6, 7, 8, 3, 1, 4)
along_z = (6, 7, 8, 5, 4, 2)
both_yz = (6, 7, 8, 4)
pairs_yz = ((1, 2), (3, 5))
time_step = 0.5


def cheb_table(node_count):
    intervals = node_count - 1
    places = np.arange(node_count)
    points = np.cos(np.pi * places / intervals)
    weights = np.where((places == 0) | (places == intervals), 2.0, 1.0)
    scaled = weights * (-1.0) ** places
    differ = points[:, None] - points[None, :] + np.eye(node_count)
    matrix = np.outer(scaled, 1.0 / scaled) / differ
    matrix = matrix - np.eye(node_count) * np.sum(matrix, axis=1)[:, None]
    return matrix / (node_count * node_count / 4.0)


def taylor_weight(degree):
    return time_step ** (degree + 1) / math.factorial(degree + 1)


def tables():
    slope = cheb_table(P_SIZE).astype(np.float32).astype(np.float64)
    high = slope.astype(ml_dtypes.bfloat16).astype(np.float64)
    low = slope - high
    one = np.eye(P_SIZE)
    two = np.eye(2)

    def spread(matrix):
        along_b = np.kron(two, np.kron(matrix.T, one))
        along_e = np.kron(two, np.kron(one, matrix.T))
        return along_b, along_e

    hy, hz = spread(high)
    ly, lz = spread(low)
    none = np.zeros_like(hy)
    w1 = np.concatenate(
        [np.concatenate([hy, hz], 1), np.concatenate([hy, hz], 1), np.concatenate([ly, lz], 1)], 0
    )
    diag_high = np.block([[hy, none], [none, hz]])
    diag_low = np.block([[ly, none], [none, lz]])
    w2 = np.concatenate([diag_high, diag_high, diag_low], 0)

    half = P_SIZE // 2
    top = slope[:half, :half]
    mirror = slope[:half, ::-1][:, :half]
    lane_half = np.arange(LANES) // HALF
    rows = []
    for part in ((top + mirror) / 2, (top - mirror) / 2):
        for t in range(2):
            for s in range(2):
                for source in (lane_half, 1 - lane_half):
                    rows.append(part[2 * t + lane_half, 2 * s + source])
    xc = np.broadcast_to(np.stack(rows)[:, None, :], (len(rows), SUB, LANES))
    return (
        jnp.asarray(w1.astype(ml_dtypes.bfloat16)),
        jnp.asarray(w2.astype(ml_dtypes.bfloat16)),
        jnp.asarray(np.ascontiguousarray(xc).astype(np.float32)),
    )


def face_tables():
    node = np.arange(P_SIZE**3)
    places = (node // P_SIZE % P_SIZE, node % P_SIZE)
    others = (
        node // HALF * P_SIZE + node % P_SIZE,
        (node // HALF + P_SIZE // 2) % P_SIZE * P_SIZE + node // P_SIZE % P_SIZE,
    )
    pick = np.zeros((P_SIZE**3, 2 * LANES))
    for k in range(2):
        for side, place in enumerate((0, P_SIZE - 1)):
            on = places[k] == place
            pick[node[on], k * LANES + side * HALF + others[k][on]] = 1.0
    squeeze = np.concatenate([pick, pick], 0).astype(ml_dtypes.bfloat16)
    in_first = np.arange(LANES) % HALF < HALF // 2
    both = []
    for part in range(2):
        keep_y = in_first if part == 0 else ~in_first
        mixed = np.where(keep_y[None, :], pick[:, :LANES], pick[:, LANES:])
        piece = mixed[part * 2 * LANES : (part + 1) * 2 * LANES].T
        both += [piece, piece]
    spread = np.concatenate(both, 0).astype(ml_dtypes.bfloat16)
    return jnp.asarray(squeeze), jnp.asarray(spread)


def roll(value, by):
    by = by % LANES
    return value if by == 0 else pltpu.roll(value, by, value.ndim - 1)


def lane_ids(rows):
    return lax.broadcasted_iota(jnp.int32, (rows, LANES), 1)


def split(value):
    high = value.astype(jnp.bfloat16)
    return high, (value - high.astype(jnp.float32)).astype(jnp.bfloat16)


def turn(load, r):
    return [[roll(load(f, r, SUB, t), HALF) for t in range(TILES)] for f in along_x]


def x_slope(own, other, xc_ref):
    sums = [[], []]
    for kind in range(2):
        sources = []
        for s in range(2):
            if kind == 0:
                sources.append((own[s] + other[3 - s], other[s] + own[3 - s]))
            else:
                sources.append((own[s] - other[3 - s], other[s] - own[3 - s]))
        for t in range(2):
            total = None
            for s in range(2):
                for swap in range(2):
                    term = sources[s][swap] * xc_ref[((kind * 2 + t) * 2 + s) * 2 + swap]
                    total = term if total is None else total + term
            sums[kind].append(total)
    slopes = [None] * TILES
    for t in range(2):
        even, odd = sums[0][t], sums[1][t]
        slopes[t] = even + odd
        slopes[3 - t] = roll(odd - even, HALF)
    return slopes


def begin_operator(split_rows, tabs, first, rows, exact):
    w1_ref, w2_ref, _ = tabs
    left, right = [], []
    for r in range(first, first + rows, PACK):
        for t in range(TILES):
            parts = {f: split_rows(f, r, PACK, t) for f in both_yz + pairs_yz[0] + pairs_yz[1]}
            for f in both_yz:
                high, low = parts[f]
                left.append(jnp.concatenate([high, low, high], 1) if exact else high)
            for f, g in pairs_yz:
                (high_f, low_f), (high_g, low_g) = parts[f], parts[g]
                pair = [high_f, high_g]
                right.append(jnp.concatenate(pair + [low_f, low_g] + pair if exact else pair, 1))
    left, right = jnp.concatenate(left, 0), jnp.concatenate(right, 0)
    return (
        jnp.dot(left, w1_ref[: left.shape[1]], preferred_element_type=jnp.float32),
        jnp.dot(right, w2_ref[: right.shape[1]], preferred_element_type=jnp.float32),
    )


def end_operator(load, material, tabs, products, first, rows, scale, emit):
    xc_ref = tabs[2]
    o1, o2 = products

    def yz(values, count, i, t, r):
        at = (((r - first) // PACK * TILES + t) * count + i) * PACK + r % PACK
        return values[at : at + SUB, :LANES], values[at : at + SUB, LANES:]

    following = turn(load, first)
    for r in range(first, first + rows, SUB):
        turned = following
        if r + SUB < first + rows:
            following = turn(load, r + SUB)
        slopes = [
            x_slope([load(f, r, SUB, t) for t in range(TILES)], turned[i], xc_ref) for i, f in enumerate(along_x)
        ]
        factor = scale(r)
        for t in range(TILES):
            lame, shear, light = [m if factor is None else m * factor for m in material(r, t)]
            shear_2 = shear + shear
            dy_vx, dz_vx = yz(o1, 4, 0, t, r)
            dy_vy, dz_vy = yz(o1, 4, 1, t, r)
            dy_vz, dz_vz = yz(o1, 4, 2, t, r)
            dy_syz, dz_syz = yz(o1, 4, 3, t, r)
            dy_syy, dz_szz = yz(o2, 2, 0, t, r)
            dy_sxy, dz_sxz = yz(o2, 2, 1, t, r)
            dx_vx, dx_vy, dx_vz, dx_sxx, dx_sxy, dx_sxz = (slope[t] for slope in slopes)
            diverge = lame * (dx_vx + dy_vy + dz_vz)
            emit(0, r, t, diverge + shear_2 * dx_vx)
            emit(1, r, t, diverge + shear_2 * dy_vy)
            emit(2, r, t, diverge + shear_2 * dz_vz)
            emit(3, r, t, shear * (dy_vx + dx_vy))
            emit(4, r, t, shear * (dz_vy + dy_vz))
            emit(5, r, t, shear * (dz_vx + dx_vz))
            emit(6, r, t, light * (dx_sxx + dy_sxy + dz_sxz))
            emit(7, r, t, light * (dx_sxy + dy_syy + dz_syz))
            emit(8, r, t, light * (dx_sxz + dy_syz + dz_szz))


def apply_operator(load, split_rows, material, tabs, rows, size, scale, emit, exact=True):
    groups = range(0, rows, size)
    products = [begin_operator(split_rows, tabs, first, size, exact) for first in groups]
    for first, product in zip(groups, products):
        end_operator(load, material, tabs, product, first, size, scale, emit)


def span(tile):
    return slice(tile * LANES, (tile + 1) * LANES)


def pack_faces(read, rows):
    low = lane_ids(rows // 2) < HALF
    first, second = read(0, 0), read(rows // 2, 0)
    start = jnp.where(low, first, roll(second, HALF))
    first, second = read(0, 3), read(rows // 2, 3)
    end = jnp.where(low, roll(first, HALF), second)
    return end, start


def odd_device():
    return lax.rem(lax.axis_index("space"), 2) == 1


def send_faces(odd, near_ref, far_ref, index, end, start):
    near_ref[index] = jnp.where(odd, end, start)
    far_ref[index] = jnp.where(odd, start, end)


def got_faces(odd, near_ref, far_ref, index):
    near, far = near_ref[index], far_ref[index]
    return jnp.where(odd, far, near), jnp.where(odd, near, far)


def wave_speed(density, lame, shear):
    return jnp.sqrt((lame + 2.0 * shear) / density)


def early_kernel(*refs):
    sources, targets = refs[:LOADED], refs[LOADED : 2 * LOADED]
    out_ref, far_ref, near_ref = refs[2 * LOADED : 2 * LOADED + 3]
    sems = refs[2 * LOADED + 3]
    sol_ref, mat_ref, w1_ref, w2_ref, xc_ref = targets[:5]
    rows = out_ref.shape[1]
    upper, lower = pl.ds(rows, rows), pl.ds(0, rows)
    pairs = [(sources[i].at[:, upper, :], targets[i].at[:, upper, :]) for i in range(2)]
    pairs += [(sources[i], targets[i]) for i in range(2, 5)]
    pairs += [(sources[i].at[:, lower, :], targets[i].at[:, lower, :]) for i in range(2)]
    pairs += [(sources[i], targets[i]) for i in range(5, LOADED)]
    copies = [pltpu.make_async_copy(source, target, sems.at[i]) for i, (source, target) in enumerate(pairs)]
    for copy in copies:
        copy.start()
    for copy in copies[:5]:
        copy.wait()
    load = lambda f, r, count, t: sol_ref[f, rows + r : rows + r + count, span(t)]
    material = lambda r, t: (
        mat_ref[1, rows + r : rows + r + SUB, span(t)],
        mat_ref[2, rows + r : rows + r + SUB, span(t)],
        1.0 / mat_ref[0, rows + r : rows + r + SUB, span(t)],
    )

    def emit(f, r, t, value):
        base = time_step * load(f, r, SUB, t)
        out_ref[f, r : r + SUB, span(t)] = base + value

    split_rows = lambda f, r, count, t: split(load(f, r, count, t))
    tabs = (w1_ref, w2_ref, xc_ref)
    apply_operator(load, split_rows, material, tabs, rows, rows // 2, lambda r: taylor_weight(1), emit)
    for copy in copies[5:]:
        copy.wait()
    count = rows // 2
    odd = odd_device()
    for f in range(9):
        end, start = pack_faces(lambda r, t, f=f: out_ref[f, r : r + count, span(t)], rows)
        send_faces(odd, near_ref, far_ref, f, end, start)
    for i in range(2):

        def speed(r, t, i=i):
            return wave_speed(*[mat_ref[m, i * rows + r : i * rows + r + count, span(t)] for m in range(3)])

        end, start = pack_faces(speed, rows)
        send_faces(odd, near_ref, far_ref, 9 + i, end, start)


def refined_kernel(
    count_ref, sol_ref, mat_ref, w1_ref, w2_ref, xc_ref, squeeze_hbm, spread_hbm,
    out_ref, far_ref, near_ref, squeeze_ref, spread_ref, state, light, sems,
):
    loads = [
        pltpu.make_async_copy(squeeze_hbm, squeeze_ref, sems.at[0]),
        pltpu.make_async_copy(spread_hbm, spread_ref, sems.at[1]),
    ]
    for copy in loads:
        copy.start()
    rows = out_ref.shape[1]
    limit = count_ref[0, 0]
    light[...] = 1.0 / mat_ref[0, :rows, :]
    tabs = (w1_ref, w2_ref, xc_ref)
    material = lambda r, t: (
        mat_ref[1, r : r + SUB, span(t)],
        mat_ref[2, r : r + SUB, span(t)],
        light[r : r + SUB, span(t)],
    )

    def next_term(source, scale, first, used, exact=True):
        load = lambda f, r, count, t: source[f, r : r + count, span(t)]
        split_rows = lambda f, r, count, t: split(load(f, r, count, t))

        def emit(f, r, t, value):
            at = pl.ds(r, SUB)
            before = time_step * sol_ref[f, at, span(t)] if first else out_ref[f, at, span(t)]
            state[f, at, span(t)] = value
            out_ref[f, at, span(t)] = before + value

        apply_operator(load, split_rows, material, tabs, used, rows // 2, scale, emit, exact)

    def term(used, exact, degree, carry):
        ratio = time_step / jnp.full((SUB, LANES), degree + 1, jnp.int32).astype(jnp.float32)

        def scale(r):
            ids = r + lax.broadcasted_iota(jnp.int32, (SUB, LANES), 0)
            return jnp.where(ids < limit, ratio, 0.0)

        next_term(state, scale, False, used, exact)
        return carry

    def terms(used):
        lax.fori_loop(2, ORD_EXACT, functools.partial(term, used, True), 0)
        lax.fori_loop(ORD_EXACT, ORD, functools.partial(term, used, False), 0)

    next_term(sol_ref, lambda r: taylor_weight(1), True, rows)

    @pl.when(limit > rows // 2)
    def _():
        terms(rows)

    @pl.when(limit <= rows // 2)
    def _():
        terms(rows // 2)

    for copy in loads:
        copy.wait()
    count = rows // 2
    odd = odd_device()
    for f in range(9):
        end, start = pack_faces(lambda r, t, f=f: out_ref[f, r : r + count, span(t)], rows)
        send_faces(odd, near_ref, far_ref, f, end, start)


def hot(row, first, count):
    cells = row.shape[1]
    ids = first + lax.broadcasted_iota(jnp.int32, (count, cells), 0)
    return jnp.where(ids == row, 1.0, 0.0).T


def hot_back(row):
    cells = row.shape[1]
    ids = lax.broadcasted_iota(jnp.int32, (cells, cells), 0)
    return jnp.where(ids == row, 1.0, 0.0).astype(jnp.bfloat16)


def unpack_faces(after, before):
    low = lane_ids(after.shape[0]) < HALF
    return jnp.concatenate(
        [
            jnp.where(low, after, 0.0),
            jnp.where(low, roll(after, HALF), 0.0),
            jnp.where(low, 0.0, roll(before, HALF)),
            jnp.where(low, 0.0, before),
        ],
        0,
    )


def flux(direction, jump, lame, shear, light, speed):
    members = ((6, 7, 8, 0, 3, 5), (6, 7, 8, 3, 1, 4), (6, 7, 8, 5, 4, 2))[direction]
    g = [jump[m] for m in members]
    through = g[direction]
    spread_out = lame * through
    normal = [spread_out, spread_out, spread_out, None, None, None, light * g[3], light * g[4], light * g[5]]
    normal[direction] = spread_out + 2.0 * (shear * through)
    if direction == 0:
        normal[3], normal[5] = shear * g[1], shear * g[2]
    elif direction == 1:
        normal[3], normal[4] = shear * g[0], shear * g[2]
    else:
        normal[4], normal[5] = shear * g[1], shear * g[0]
    return [
        speed * jump[f] if normal[f] is None else normal[f] + speed * jump[f] for f in range(9)
    ]


def correct_kernel(
    sol_ref, mat_ref, low_ref, high_ref, beside_ref, far_ref, near_ref,
    w1_ref, w2_ref, xc_ref, squeeze_ref, spread_ref,
    out_ref, ends_ref, xmat_ref, late_ref,
    pieces, compact, xfix, hot_ref, xhot, rhs, far, fix, fixed, light, fixes, middle, sems,
):
    cells = sol_ref.shape[1]
    half = low_ref.shape[1]
    nodes = sol_ref.shape[2]
    in_low = lane_ids(SUB) < HALF
    in_first = lane_ids(cells) % HALF < HALF // 2
    side = jnp.where(in_low, 0.25, -0.25)

    def integral(f, r, count, t):
        if r < half:
            return low_ref[f, r : r + count, span(t)]
        return high_ref[f, r - half : r - half + count, span(t)]

    for f in range(12):
        for start in (0, half):
            at = pl.ds(f * cells + start, half)
            for t in range(TILES):
                value = integral(f, start, half, t) if f < 9 else mat_ref[f - 9, start : start + half, span(t)]
                high, low = split(value)
                pieces[at, span(t)] = high
                pieces[at, nodes + t * LANES : nodes + (t + 1) * LANES] = low
    for f in range(0, 12, 3):
        at = pl.ds(f * cells, 3 * cells)
        compact[at, :] = jnp.dot(pieces[at, :], squeeze_ref[...], preferred_element_type=jnp.float32)
    light[...] = 1.0 / mat_ref[0]

    here = beside_ref[...] % cells
    odd = odd_device()
    for k in range(2):
        direction = k + 1
        plus = hot_back(here[2 * direction : 2 * direction + 1])
        minus = hot_back(here[2 * direction + 1 : 2 * direction + 2])
        for i, pick in enumerate((plus, minus)):
            at = pl.ds(i * cells, cells)
            hot_ref[k, at, :LANES] = pick
            hot_ref[k, at, LANES:] = pick

        def face(f, k=k):
            return compact[pl.ds(f * cells, cells), span(k)]

        for f in range(10):
            own = face(f) if f < 9 else wave_speed(face(9), face(10), face(11))
            if f == 9:
                far[k, :cells, span(10)] = own
            high, low = split(roll(own, HALF))
            rhs[k, :LANES, span(f)] = high
            rhs[k, LANES : 2 * LANES, span(f)] = low
        far[k, :, : 10 * LANES] = jnp.dot(
            hot_ref[k], rhs[k, : 2 * LANES, :], preferred_element_type=jnp.float32
        )
        for r in range(0, cells, SUB):
            at = pl.ds(r, SUB)

            def own(f, k=k, r=r):
                return compact[pl.ds(f * cells + r, SUB), span(k)]

            def across(f, k=k, r=r):
                return jnp.where(in_low, far[k, pl.ds(r, SUB), span(f)], far[k, pl.ds(cells + r, SUB), span(f)])

            jump = [across(f) - own(f) for f in range(9)]
            speed = 0.25 * jnp.maximum(across(9), far[k, at, span(10)])
            values = flux(direction, jump, side * own(10), side * own(11), side / own(9), speed)
            for f, value in enumerate(values):
                fix[pl.ds(f * cells + r, SUB), span(k)] = value
    for f in range(9):
        at = pl.ds(f * cells, cells)
        along, across = fix[at, span(0)], fix[at, span(1)]
        for k, value in enumerate((jnp.where(in_first, along, across), jnp.where(in_first, across, along))):
            high, low = split(value)
            fixed[at, span(2 * k)] = high
            fixed[at, span(2 * k + 1)] = low

    plus, minus = here[1:2], here[0:1]
    plus, minus = hot(plus, 0, cells), hot(minus, 0, cells)
    early = jnp.concatenate([plus[:, half:], minus[:, half:]], 1).astype(jnp.bfloat16)
    late = jnp.concatenate([plus[:, :half], minus[:, :half]], 1).astype(jnp.bfloat16)
    late_ref[:, :LANES] = late
    late_ref[:, LANES:] = late
    for i, pick in enumerate((early, early, late, late)):
        xhot[:, span(i)] = pick
    for f in range(9):
        high, low = split(unpack_faces(*got_faces(odd, near_ref, far_ref, f)))
        rhs[2, 0:LANES, span(f)] = high
        rhs[2, LANES : 2 * LANES, span(f)] = low
    for k, f in ((0, 10), (2, 9)):
        high, low = split(unpack_faces(*got_faces(odd, near_ref, far_ref, f)))
        rhs[2, k * LANES : (k + 1) * LANES, span(9)] = high
        rhs[2, (k + 1) * LANES : (k + 2) * LANES, span(9)] = low
    far[2, :cells, : 9 * LANES] = jnp.dot(
        xhot[:, : 2 * LANES], rhs[2, : 2 * LANES, : 9 * LANES], preferred_element_type=jnp.float32
    )
    far[2, :cells, span(9)] = jnp.dot(xhot[...], rhs[2, :, span(9)], preferred_element_type=jnp.float32)
    for r in range(0, cells, SUB):
        at = pl.ds(r, SUB)
        jump = [
            far[2, at, span(f)] - jnp.where(in_low, integral(f, r, SUB, 0), integral(f, r, SUB, 3)) for f in range(9)
        ]
        density, lame, shear = (
            jnp.where(in_low, mat_ref[m, at, span(0)], mat_ref[m, at, span(3)]) for m in range(3)
        )
        speed = 0.25 * jnp.maximum(far[2, at, span(9)], wave_speed(density, lame, shear))
        lame, shear, weight = side * lame, side * shear, side / density
        for f, value in enumerate(flux(0, jump, lame, shear, weight, speed)):
            xfix[f, at, :] = value
        for i, value in enumerate((lame, shear, weight, speed)):
            xmat_ref[i, at, :] = value

    for k in range(2):
        at = slice(2 * k * LANES, 2 * (k + 1) * LANES)
        fixes[:, at] = jnp.dot(fixed[:, at], spread_ref[at, :], preferred_element_type=jnp.float32)

    def split_rows(f, r, count, t):
        at = pl.ds(f * cells + r, count)
        return pieces[at, span(t)], pieces[at, nodes + t * LANES : nodes + (t + 1) * LANES]

    def material(r, t):
        at = pl.ds(r, SUB)
        return mat_ref[1, at, span(t)], mat_ref[2, at, span(t)], light[at, span(t)]

    def emit(f, r, t, value):
        at = pl.ds(r, SUB)
        total = sol_ref[f, at, span(t)] + value + fixes[pl.ds(f * cells + r, SUB), span(t)]
        if t == 0:
            ends_ref[0, f, at, :] = total + jnp.where(in_low, xfix[f, at, :], 0.0)
        elif t == TILES - 1:
            ends_ref[1, f, at, :] = total + jnp.where(in_low, 0.0, xfix[f, at, :])
        else:
            middle[f, at, span(t - 1)] = total
        if f == 8 and t == TILES - 1 and (r + SUB) % half == 0:
            stores[r // half].start()

    between = pl.ds(LANES, (TILES - 2) * LANES)
    stores = [
        pltpu.make_async_copy(
            middle.at[:, pl.ds(start, half), :], out_ref.at[:, pl.ds(start, half), between], sems.at[i]
        )
        for i, start in enumerate(range(0, cells, half))
    ]
    tabs = (w1_ref, w2_ref, xc_ref)
    apply_operator(integral, split_rows, material, tabs, cells, half, lambda r: None, emit)
    for copy in stores:
        copy.wait()


def finish_kernel(done_ref, ends_ref, far_ref, near_ref, xmat_ref, late_ref, out_ref, ends, rhs, far, sems):
    del done_ref
    cells = ends.shape[2]
    odd = odd_device()
    for f in range(9):
        high, low = split(unpack_faces(*got_faces(odd, near_ref, far_ref, f)))
        rhs[0:LANES, span(f)] = high
        rhs[LANES : 2 * LANES, span(f)] = low
    for f in range(0, 9, 3):
        columns = slice(f * LANES, (f + 3) * LANES)
        far[:, columns] = jnp.dot(late_ref[...], rhs[:, columns], preferred_element_type=jnp.float32)
    in_low = lane_ids(SUB) < HALF
    size = cells // sems.shape[1]
    stores = []
    for r in range(0, cells, SUB):
        at = pl.ds(r, SUB)
        jump = [far[at, span(f)] for f in range(9)]
        lame, shear, weight, speed = (xmat_ref[i, at, :] for i in range(4))
        for f, value in enumerate(flux(0, jump, lame, shear, weight, speed)):
            ends[0, f, at, :] = ends_ref[0, f, at, :] + jnp.where(in_low, value, 0.0)
            ends[1, f, at, :] = ends_ref[1, f, at, :] + jnp.where(in_low, 0.0, value)
        if (r + SUB) % size == 0:
            part = pl.ds(r + SUB - size, size)
            for i, t in enumerate((0, TILES - 1)):
                copy = pltpu.make_async_copy(
                    ends.at[i, :, part, :], out_ref.at[:, part, pl.ds(t * LANES, LANES)], sems.at[i, r // size]
                )
                copy.start()
                stores.append(copy)
    for copy in stores:
        copy.wait()


def exchange(near, far):
    peers = lax.axis_size("space")
    got_near = lax.ppermute(near, "space", [(i, i + (-1 if i % 2 else 1)) for i in range(peers)])
    got_far = lax.ppermute(far, "space", [(i, (i + (1 if i % 2 else -1)) % peers) for i in range(peers)])
    return got_near, got_far


def f32(*shape):
    return jax.ShapeDtypeStruct(shape, jnp.float32)


def on_device(solution, material, neighbours, refine_count):
    cells, nodes = solution.shape[1:]
    rows = REF_MAX
    params = lambda mib: pltpu.CompilerParams(vmem_limit_bytes=mib * 1024 * 1024)
    early_shape, late_shape = (11, rows // 2, LANES), (9, rows // 2, LANES)
    in_vmem = pl.BlockSpec(memory_space=pltpu.VMEM)
    in_hbm = pl.BlockSpec(memory_space=pltpu.HBM)

    sources = (solution, material) + tables()
    pinned = lambda arrays: [pltpu.with_memory_space_constraint(x, pltpu.HBM) for x in arrays]
    faces = face_tables()
    *loaded, high, far, near = pl.pallas_call(
        early_kernel,
        in_specs=[in_hbm] * LOADED,
        out_specs=[in_vmem] * (LOADED + 3),
        out_shape=[pltpu.VMEM(x.shape, x.dtype) for x in sources]
        + [pltpu.VMEM((9, rows, nodes), jnp.float32), f32(*early_shape), f32(*early_shape)],
        scratch_shapes=[pltpu.SemaphoreType.DMA((LOADED + 2,))],
        compiler_params=params(20),
        name="early",
    )(*pinned(sources))
    sol, mat, w1, w2, xc = loaded
    early_near, early_far = exchange(near, far)

    low, far, near, squeeze, spread = pl.pallas_call(
        refined_kernel,
        in_specs=[pl.BlockSpec(memory_space=pltpu.SMEM)] + [in_vmem] * 5 + [in_hbm] * 2,
        out_specs=[in_vmem] * 5,
        out_shape=[pltpu.VMEM((9, rows, nodes), jnp.float32), f32(*late_shape), f32(*late_shape)]
        + [pltpu.VMEM(x.shape, x.dtype) for x in faces],
        scratch_shapes=[
            pltpu.VMEM((9, rows, nodes), jnp.float32),
            pltpu.VMEM((rows, nodes), jnp.float32),
            pltpu.SemaphoreType.DMA((2,)),
        ],
        compiler_params=params(20),
        name="refined",
    )(refine_count, sol, mat, w1, w2, xc, *pinned(faces))
    late_near, late_far = exchange(near, far)

    done, ends, xmat, late_hot = pl.pallas_call(
        correct_kernel,
        in_specs=[in_vmem] * 12,
        out_specs=[in_hbm] + [in_vmem] * 3,
        out_shape=[
            pltpu.HBM(solution.shape, jnp.float32),
            pltpu.VMEM((2, 9, cells, LANES), jnp.float32),
            pltpu.VMEM((4, cells, LANES), jnp.float32),
            pltpu.VMEM((cells, 2 * LANES), jnp.bfloat16),
        ],
        scratch_shapes=[
            pltpu.VMEM((12 * cells, 2 * nodes), jnp.bfloat16),
            pltpu.VMEM((12 * cells, 2 * LANES), jnp.float32),
            pltpu.VMEM((9, cells, LANES), jnp.float32),
            pltpu.VMEM((2, 2 * cells, 2 * LANES), jnp.bfloat16),
            pltpu.VMEM((cells, 4 * LANES), jnp.bfloat16),
            pltpu.VMEM((3, 4 * LANES, 10 * LANES), jnp.bfloat16),
            pltpu.VMEM((3, 2 * cells, 11 * LANES), jnp.float32),
            pltpu.VMEM((9 * cells, 2 * LANES), jnp.float32),
            pltpu.VMEM((9 * cells, 4 * LANES), jnp.bfloat16),
            pltpu.VMEM((cells, nodes), jnp.float32),
            pltpu.VMEM((9 * cells, nodes), jnp.float32),
            pltpu.VMEM((9, cells, nodes - 2 * LANES), jnp.float32),
            pltpu.SemaphoreType.DMA((2,)),
        ],
        compiler_params=params(40),
        name="correct",
    )(sol, mat, low, high, neighbours, early_far, early_near, w1, w2, xc, squeeze, spread)

    return pl.pallas_call(
        finish_kernel,
        in_specs=[in_hbm] + [in_vmem] * 5,
        out_specs=in_hbm,
        out_shape=f32(*solution.shape),
        scratch_shapes=[
            pltpu.VMEM((2, 9, cells, LANES), jnp.float32),
            pltpu.VMEM((2 * LANES, 9 * LANES), jnp.bfloat16),
            pltpu.VMEM((cells, 9 * LANES), jnp.float32),
            pltpu.SemaphoreType.DMA((2, 4)),
        ],
        input_output_aliases={0: 0},
        compiler_params=params(8),
        name="finish",
    )(done, ends, late_far, late_near, xmat, late_hot)


def solution(mesh):
    in_specs = (
        P(None, ("space", "help"), None),
        P(None, ("space", "help"), None),
        P(None, ("space", "help")),
        P("space", "help"),
    )
    out_specs = P(None, ("space", "help"), None)
    return jax.shard_map(
        on_device, mesh=mesh, in_specs=in_specs, out_specs=out_specs, check_vma=False
    )
```
